256 devices in a mesh: rows: 64 (over z, y, core), help: 4 (over x).
Axes of the slice: x: 4, y: 4, z: 8, core: 2. Of those that a mesh axis runs over, the one named last changes fastest.
Arguments:
- panel: bfloat16 [32, 262144], P(None, ('rows', 'help')), may hold values from -6 to 6
- tiles: bfloat16 [2, 2048, 16, 128, 128], P(None, ('rows', 'help')), may hold values from -0.125 to 0.125
- tile_cols: int32 [2048, 16], P(('rows', 'help')), may hold values from 0 to 63
- tile_count: int32 [2048], P(('rows', 'help')), may hold values from 4 to 16
- row_assign: int32 [2048], P('rows'), may hold values from 0 to 31, as said below
- send_lists: int32 [64, 2, 16], P('rows'), may hold values from 0 to 31, as said below
- centers: float32 [2], replicated, may hold values from -0.5 to 0.5
- half_widths: float32 [2], replicated, may hold values from 0.6 to 1.5
Outputs:
- filtered: bfloat16 [2, 32, 262144], P(None, None, ('rows', 'help'))
- gram: float32 [2, 2, 32, 32], replicated
The draws below stay inside these ranges and needn't reach their ends.
Inputs may be any that keep to these rules, and one draw needn't show every extreme that they name: `row_assign`: each aligned group of 32 entries (one slab) is a permutation of 0 to 31. `send_lists`: the 16 entries of each list are distinct tile rows of the slab.
All inputs are finite; a program needn't handle non-finite values.
Results may differ from the reference program's by a relative error of at most 0.0042.
Values may be sent and summed in bfloat16 or wider, within the bound.
No kernel may reach another device: no remote copies, remote signals or barrier semaphores. Data moves between devices by JAX's collectives and lax.ppermute only.
A program may use at most 64 MiB of HBM per device.

```python
import math
import jax
import jax.numpy as jnp
from jax import lax

VOLUMES = 2
VECTORS = 32
TILE_SIDE = 128
TILE_SLOTS = 16
SLAB_TILES = 32
GHOSTS = 16
SLABS = 64
BLOCKS = 2048
N_ROWS = 64


def draw_row_assign(key, part):
    key = jax.random.fold_in(key, 11)
    slab_keys = jax.random.split(key, N_ROWS)
    orders = jax.vmap(lambda slab_key: jax.random.permutation(slab_key, SLAB_TILES))(slab_keys)
    return orders.reshape(BLOCKS).astype(jnp.int32)


def draw_send_lists(key, part):
    key = jax.random.fold_in(key, 12)
    list_keys = jax.random.split(key, N_ROWS * 2)
    orders = jax.vmap(lambda list_key: jax.random.permutation(list_key, SLAB_TILES)[:GHOSTS])(list_keys)
    return orders.reshape(N_ROWS, 2, GHOSTS).astype(jnp.int32)


def place_ends(values, own_key, smallest, largest):
    longest = values.shape.index(max(values.shape))
    spots = []
    for shift in (0, 1):
        where = [jax.random.randint(jax.random.fold_in(own_key, axis), (), 0, length) for axis, length in enumerate(values.shape)]
        where[longest] = (where[longest] + shift) % values.shape[longest]
        spots.append(tuple(where))
    return values.at[spots[0]].set(smallest).at[spots[1]].set(largest)


def shard_levels(stream_key, dims, pieces, smallest, top_value):
    gain = 1.0
    for position, blocks in pieces:
        draws = jax.random.uniform(jax.random.fold_in(jax.random.fold_in(stream_key, 6), position), (blocks,), jnp.float32, smallest / len(pieces), top_value / len(pieces))
        gain = gain * jnp.repeat(jnp.exp(draws), dims[position] // blocks).reshape((-1,) + (1,) * (len(dims) - 1 - position))
    return gain


def centred(stream_key, extent, scale, limit, shards=(), held_as=jnp.bfloat16):
    drawn = scale * jax.random.normal(stream_key, extent, jnp.float32)
    if shards:
        drawn = drawn * shard_levels(stream_key, extent, shards, -0.22, 0.18)
    return jnp.clip(drawn, -limit, limit).astype(held_as)


def setup_inputs(seed: int = 0) -> dict:
    keys = jax.random.split(jax.random.key(seed), 9)
    return {
        "panel": centred(keys[0], (VECTORS, BLOCKS * TILE_SIDE), 1.0, 6.0, ((1, 256),)),
        "tiles": centred(keys[1], (VOLUMES, BLOCKS, TILE_SLOTS, TILE_SIDE, TILE_SIDE), (TILE_SLOTS * TILE_SIDE) ** -0.5, 0.125, ((1, 256),)),
        "tile_cols": place_ends(jax.random.randint(keys[2], (BLOCKS, TILE_SLOTS), 0, SLAB_TILES + 2 * GHOSTS), jax.random.fold_in(keys[2], 1), 0, (SLAB_TILES + 2 * GHOSTS) - 1).astype(jnp.int32),
        "tile_count": place_ends(jax.random.randint(keys[3], (BLOCKS,), max(1, TILE_SLOTS // 4), TILE_SLOTS + 1), jax.random.fold_in(keys[3], 1), max(1, TILE_SLOTS // 4), TILE_SLOTS).astype(jnp.int32),
        "row_assign": draw_row_assign(jax.random.fold_in(keys[8], 71), 0),
        "send_lists": draw_send_lists(jax.random.fold_in(keys[8], 71), 0),
        "centers": jnp.clip(jax.random.uniform(keys[6], (VOLUMES,), jnp.float32, -0.5, 0.5), -0.5, 0.5),
        "half_widths": jnp.clip(jnp.exp(jax.random.uniform(keys[7], (VOLUMES,), jnp.float32, math.log(0.6), math.log(1.5))), 0.6, 1.5),
    }


def extend_slabs(blocks, send_lists):
    left_idx = send_lists[:, 1, :].astype(jnp.int32)
    right_idx = send_lists[:, 0, :].astype(jnp.int32)
    to_next = jnp.take_along_axis(blocks, left_idx[None, None, :, :, None], axis=3)
    to_prev = jnp.take_along_axis(blocks, right_idx[None, None, :, :, None], axis=3)
    from_left = jnp.roll(to_next, 1, axis=2)
    from_right = jnp.roll(to_prev, -1, axis=2)
    return jnp.concatenate([blocks, from_left, from_right], axis=3)


def apply_tiles(extended, tiles_slab, cols_slab, live_slab):
    ext_first = jnp.moveaxis(extended, 2, 0)
    tiles_first = jnp.moveaxis(tiles_slab, 1, 0)

    def one_slab(items):
        ext_one, tile_one, col_one, live_one = items
        picked = ext_one[:, :, col_one, :]
        picked = jnp.where(live_one[None, None, :, :, None], picked, jnp.zeros((), picked.dtype))
        return jnp.einsum("vpjkc,vjkrc->vpjr", picked, tile_one.astype(jnp.float32))

    result = lax.map(one_slab, (ext_first, tiles_first, cols_slab, live_slab))
    return jnp.moveaxis(result, 0, 2)


def reference(panel, tiles, tile_cols, tile_count, row_assign, send_lists, centers, half_widths):
    assign = row_assign.reshape(SLABS, SLAB_TILES).astype(jnp.int32)
    inverse = jnp.argsort(assign, axis=1).astype(jnp.int32)
    cols_slab = tile_cols.reshape(SLABS, SLAB_TILES, TILE_SLOTS).astype(jnp.int32)
    counts = tile_count.reshape(SLABS, SLAB_TILES)
    live_slab = jnp.arange(TILE_SLOTS, dtype=jnp.int32)[None, None, :] < counts[:, :, None]
    tiles_slab = tiles.reshape(VOLUMES, SLABS, SLAB_TILES, TILE_SLOTS, TILE_SIDE, TILE_SIDE)
    base = panel.astype(jnp.float32).reshape(VECTORS, SLABS, SLAB_TILES, TILE_SIDE)
    x_nat = jnp.broadcast_to(base[None], (VOLUMES,) + base.shape)
    x_store = jnp.take_along_axis(x_nat, assign[None, None, :, :, None], axis=3)
    centre = centers[:, None, None, None, None]
    spread = half_widths[:, None, None, None, None]
    first_h = apply_tiles(extend_slabs(x_nat, send_lists), tiles_slab, cols_slab, live_slab)
    first = ((first_h - centre * x_store) / spread).astype(jnp.bfloat16)
    first_f = first.astype(jnp.float32)
    first_nat = jnp.take_along_axis(first_f, inverse[None, None, :, :, None], axis=3)
    second_h = apply_tiles(extend_slabs(first_nat, send_lists), tiles_slab, cols_slab, live_slab)
    second = (2.0 * (second_h - centre * first_f) / spread - x_store).astype(jnp.bfloat16)
    second_f = second.astype(jnp.float32)
    total = BLOCKS * TILE_SIDE
    gram_one = jnp.einsum("vpsjr,vqsjr->vpq", first_f, first_f) / total
    gram_two = jnp.einsum("vpsjr,vqsjr->vpq", second_f, second_f) / total
    second_nat = jnp.take_along_axis(second_f, inverse[None, None, :, :, None], axis=3)
    filtered = second_nat.reshape(VOLUMES, VECTORS, BLOCKS * TILE_SIDE).astype(jnp.bfloat16)
    gram = jnp.stack([gram_one, gram_two], axis=1)
    return filtered, gram
```

```python
import functools

import jax
import jax.numpy as jnp
from jax import lax
from jax.experimental import pallas as pl
from jax.experimental.pallas import tpu as pltpu
from jax.sharding import PartitionSpec as P

CORES = 2
SIDE_CHIPS = 4
NT = (((1,), (1,)), ((), ()))
VMEM = pl.BlockSpec(memory_space=pltpu.VMEM)
SMEM = pl.BlockSpec(memory_space=pltpu.SMEM)


def spread_panel(helpers, lists, *refs):
    shards, (slab, to_pair, to_cross) = refs[:helpers], refs[helpers:]
    me = lax.axis_index("help")
    odd = lax.rem(lax.axis_index("rows"), 2)
    side = slab.shape[2]
    row_tiles = slab.shape[0] // helpers
    for d in range(helpers):
        base = (me ^ d) * row_tiles
        for j in range(row_tiles):
            slab[base + j] = shards[d][:, j * side:(j + 1) * side]
    for g in range(to_pair.shape[0]):
        to_pair[g] = slab[lists[0, 1 - odd, g]]
        to_cross[g] = slab[lists[0, odd, g]]


def spread_field(helpers, lists, assign, *refs):
    shards, (slab, to_pair, to_cross) = refs[:helpers], refs[helpers:]
    me = lax.axis_index("help")
    odd = lax.rem(lax.axis_index("rows"), 2)
    row_tiles = slab.shape[1] // helpers
    for d in range(helpers):
        base = (me ^ d) * row_tiles
        for j in range(row_tiles):
            slab[:, assign[base + j]] = shards[d][:, j]
    for g in range(to_pair.shape[1]):
        to_pair[:, g] = slab[:, lists[0, 1 - odd, g]]
        to_cross[:, g] = slab[:, lists[0, odd, g]]


def place_field(helpers, assign, *refs):
    shards, (out, natural) = refs[:helpers], refs[helpers:]
    me = lax.axis_index("help")
    row_tiles = natural.shape[1] // helpers
    side = natural.shape[3]
    for d in range(helpers):
        base = (me ^ d) * row_tiles
        for j in range(row_tiles):
            natural[:, assign[base + j]] = shards[d][:, j]
    for j in range(row_tiles):
        out[:, :, j * side:(j + 1) * side] = natural[:, me * row_tiles + j]


def tile_pair(tiles, j, k):
    return jnp.concatenate(
        [jnp.concatenate([tiles[v, j, k], tiles[v, j, k + 1]], axis=1) for v in range(tiles.shape[0])],
        axis=0,
    )


def apply_first(cols, count, assign, centers, widths, slab, pair, cross, tiles, first, gram, ext):
    volumes, row_tiles, slots, side, _ = tiles.shape
    slab_size = slab.shape[0]
    ghosts = pair.shape[0]
    vectors = slab.shape[1]
    me = lax.axis_index("help")
    odd = lax.rem(lax.axis_index("rows"), 2)
    ext[pl.ds(0, slab_size)] = slab[...]
    ext[pl.ds(slab_size + (1 - odd) * ghosts, ghosts)] = pair[...]
    ext[pl.ds(slab_size + odd * ghosts, ghosts)] = cross[...]
    for j in range(row_tiles):
        total = jnp.zeros((vectors, volumes * side), jnp.float32)
        for k in range(0, slots, 2):
            left = jnp.concatenate(
                [jnp.where(q < count[j], ext[cols[j, q]], 0).astype(ext.dtype) for q in (k, k + 1)], axis=1
            )
            total += lax.dot_general(left, tile_pair(tiles, j, k), NT, preferred_element_type=jnp.float32)
        stored = slab[assign[me * row_tiles + j]].astype(jnp.float32)
        for v in range(volumes):
            h = total[:, v * side:(v + 1) * side]
            first[v, j] = ((h - centers[v] * stored) / widths[v]).astype(first.dtype)
    for v in range(volumes):
        field = jnp.concatenate([first[v, j] for j in range(row_tiles)], axis=1)
        gram[v] = lax.dot_general(field, field, NT, preferred_element_type=jnp.float32)


def apply_second(
    cols, count, assign, centers, widths, base, slab, pair, cross, tiles, first, gram_one, second, gram, ext
):
    volumes, row_tiles, slots, side, _ = tiles.shape
    slab_size = slab.shape[1]
    ghosts = pair.shape[1]
    vectors = slab.shape[2]
    me = lax.axis_index("help")
    odd = lax.rem(lax.axis_index("rows"), 2)
    ext[:, pl.ds(0, slab_size)] = slab[...]
    ext[:, pl.ds(slab_size + (1 - odd) * ghosts, ghosts)] = pair[...]
    ext[:, pl.ds(slab_size + odd * ghosts, ghosts)] = cross[...]
    for j in range(row_tiles):
        total = jnp.zeros((volumes * vectors, volumes * side), jnp.float32)
        for k in range(0, slots, 2):
            left = jnp.concatenate(
                [
                    jnp.concatenate(
                        [
                            jnp.where(q < count[j], ext[v, cols[j, q]], 0).astype(ext.dtype)
                            for q in (k, k + 1)
                        ],
                        axis=1,
                    )
                    for v in range(volumes)
                ],
                axis=0,
            )
            total += lax.dot_general(left, tile_pair(tiles, j, k), NT, preferred_element_type=jnp.float32)
        stored = base[assign[me * row_tiles + j]].astype(jnp.float32)
        for v in range(volumes):
            h = total[v * vectors:(v + 1) * vectors, v * side:(v + 1) * side]
            inner = h - centers[v] * first[v, j].astype(jnp.float32)
            second[v, j] = (2.0 * inner / widths[v] - stored).astype(second.dtype)
    parts = [gram_one[v] for v in range(volumes)]
    for v in range(volumes):
        field = jnp.concatenate([second[v, j] for j in range(row_tiles)], axis=1)
        parts.append(lax.dot_general(field, field, NT, preferred_element_type=jnp.float32))
    gram[...] = jnp.concatenate(parts, axis=1)


def swapped(value, pairs):
    return lax.ppermute(value, ("rows", "help"), pairs)


def per_device(panel, tiles, tile_cols, tile_count, row_assign, send_lists, centers, half_widths):
    helpers = lax.axis_size("help")
    rows = lax.axis_size("rows")
    volumes, row_tiles, slots, side, _ = tiles.shape
    vectors = panel.shape[0]
    ghosts = send_lists.shape[2]
    slab_size = row_tiles * helpers
    bf16 = panel.dtype
    depth = rows // (SIDE_CHIPS * CORES)

    def at(z, y, core, x):
        return ((z * SIDE_CHIPS + y) * CORES + core) * helpers + x

    def shape(*dims):
        return jax.ShapeDtypeStruct(dims, bf16)

    def gathered(shard):
        others = [
            lax.ppermute(shard, "help", [(i, i ^ d) for i in range(helpers)]) for d in range(1, helpers)
        ]
        return [shard] + others

    def exchanged(to_pair, to_cross):
        cross_pairs = [(s, (s + 1) % rows if s % 2 else (s - 1) % rows) for s in range(rows)]
        cross = lax.ppermute(to_cross, "rows", cross_pairs)
        pair = lax.ppermute(to_pair, "rows", [(s, s ^ 1) for s in range(rows)])
        return pair, cross

    params = pltpu.CompilerParams(vmem_limit_bytes=24 * 1024 * 1024)

    base, to_pair, to_cross = pl.pallas_call(
        functools.partial(spread_panel, helpers),
        out_shape=[shape(slab_size, vectors, side)] + [shape(ghosts, vectors, side)] * 2,
        in_specs=[SMEM] + [VMEM] * helpers,
        out_specs=[VMEM] * 3,
        compiler_params=params,
        name="spread_panel",
    )(send_lists, *gathered(panel))
    pair, cross = exchanged(to_pair, to_cross)
    first, gram_one = pl.pallas_call(
        apply_first,
        out_shape=[
            shape(volumes, row_tiles, vectors, side),
            jax.ShapeDtypeStruct((volumes, vectors, vectors), jnp.float32),
        ],
        in_specs=[SMEM] * 5 + [VMEM] * 4,
        out_specs=[VMEM] * 2,
        scratch_shapes=[pltpu.VMEM((slab_size + 2 * ghosts, vectors, side), bf16)],
        compiler_params=params,
        name="apply_first",
    )(tile_cols, tile_count, row_assign, centers, half_widths, base, pair, cross, tiles)
    slab, to_pair, to_cross = pl.pallas_call(
        functools.partial(spread_field, helpers),
        out_shape=[shape(volumes, slab_size, vectors, side)] + [shape(volumes, ghosts, vectors, side)] * 2,
        in_specs=[SMEM] * 2 + [VMEM] * helpers,
        out_specs=[VMEM] * 3,
        compiler_params=params,
        name="spread_field",
    )(send_lists, row_assign, *gathered(first))
    pair, cross = exchanged(to_pair, to_cross)
    second, gram = pl.pallas_call(
        apply_second,
        out_shape=[
            shape(volumes, row_tiles, vectors, side),
            jax.ShapeDtypeStruct((vectors, 2 * volumes * vectors), jnp.float32),
        ],
        in_specs=[SMEM] * 5 + [VMEM] * 7,
        out_specs=[VMEM] * 2,
        scratch_shapes=[pltpu.VMEM((volumes, slab_size + 2 * ghosts, vectors, side), bf16)],
        compiler_params=params,
        name="apply_second",
    )(tile_cols, tile_count, row_assign, centers, half_widths, base, slab, pair, cross, tiles, first, gram_one)

    every = [(z, y, x) for z in range(depth) for y in range(SIDE_CHIPS) for x in range(helpers)]
    gram = gram + swapped(gram, [(at(z, y, 0, x), at(z, y, 1, x)) for z, y, x in every])
    gram = gram + sum(
        swapped(gram, [(at(z, y, 1, d), at(z, y, 1, 0)) for z in range(depth) for y in range(SIDE_CHIPS)])
        for d in range(1, helpers)
    )
    gram = gram + sum(
        swapped(gram, [(at(z, d, 1, 0), at(z, 0, 1, 0)) for z in range(depth)]) for d in range(1, SIDE_CHIPS)
    )
    gram = gram + sum(swapped(gram, [(at(d, 0, 1, 0), at(0, 0, 1, 0))]) for d in range(1, depth))

    second, gram = lax.optimization_barrier((second, gram))
    shards = gathered(second)

    own = lax.axis_index("rows") * helpers + lax.axis_index("help")
    gram = jnp.where(own == at(0, 0, 1, 0), gram, 0.0)
    gram = gram + sum(swapped(gram, [(at(0, 0, 1, 0), at(d, 0, 1, 0))]) for d in range(1, depth))
    gram = gram + sum(
        swapped(gram, [(at(z, 0, 1, 0), at(z, d, 1, 0)) for z in range(depth)]) for d in range(1, SIDE_CHIPS)
    )
    gram = gram + sum(
        swapped(gram, [(at(z, y, 1, 0), at(z, y, 1, d)) for z in range(depth) for y in range(SIDE_CHIPS)])
        for d in range(1, helpers)
    )
    gram = gram + swapped(gram, [(at(z, y, 1, x), at(z, y, 0, x)) for z, y, x in every])

    filtered = pl.pallas_call(
        functools.partial(place_field, helpers),
        out_shape=shape(volumes, vectors, row_tiles * side),
        in_specs=[SMEM] + [VMEM] * helpers,
        out_specs=VMEM,
        scratch_shapes=[pltpu.VMEM((volumes, slab_size, vectors, side), bf16)],
        compiler_params=params,
        name="place_field",
    )(row_assign, *shards)
    gram = gram.reshape(vectors, 2, volumes, vectors).transpose(2, 1, 0, 3)
    return filtered, gram / (row_tiles * side * helpers * rows)


def solution(mesh):
    placed = (
        P(None, ("rows", "help")),
        P(None, ("rows", "help"), None, None, None),
        P(("rows", "help"), None),
        P(("rows", "help")),
        P("rows"),
        P("rows", None, None),
        P(),
        P(),
    )
    return jax.shard_map(
        per_device,
        mesh=mesh,
        in_specs=placed,
        out_specs=(P(None, None, ("rows", "help")), P()),
        check_vma=False,
    )
```

```python
import functools

import jax
import jax.numpy as jnp
from jax import lax
from jax.experimental import pallas as pl
from jax.experimental.pallas import tpu as pltpu
from jax.sharding import PartitionSpec as P

CORES = 2
LANES = 128
SIDE_CHIPS = 4
NT = (((1,), (1,)), ((), ()))
VMEM = pl.BlockSpec(memory_space=pltpu.VMEM)
SMEM = pl.BlockSpec(memory_space=pltpu.SMEM)


def own_blocks(panel, tiles, blocks):
    side = blocks.shape[2]
    for j in range(blocks.shape[0]):
        blocks[j] = panel[:, j * side:(j + 1) * side]


def spread_panel(helpers, ints, *refs):
    shards, (slab, to_pair, to_cross) = refs[:helpers], refs[helpers:]
    me = lax.axis_index("help")
    odd = lax.rem(lax.axis_index("rows"), 2)
    side = slab.shape[2]
    row_tiles = slab.shape[0] // helpers
    for d in range(helpers):
        base = (me ^ d) * row_tiles
        for j in range(row_tiles):
            slab[base + j] = shards[d][:, j * side:(j + 1) * side] if d else shards[0][j]
    for g in range(to_pair.shape[0]):
        to_pair[g] = slab[ints[row_tiles + 3 - odd, g]]
        to_cross[g] = slab[ints[row_tiles + 2 + odd, g]]


def spread_field(helpers, ints, *refs):
    shards, (slab, to_pair, to_cross) = refs[:helpers], refs[helpers:]
    me = lax.axis_index("help")
    odd = lax.rem(lax.axis_index("rows"), 2)
    row_tiles = slab.shape[1] // helpers
    for d in range(helpers):
        base = (me ^ d) * row_tiles
        for j in range(row_tiles):
            slab[:, ints[row_tiles + 1, base + j]] = shards[d][:, j]
    for g in range(to_pair.shape[1]):
        to_pair[:, g] = slab[:, ints[row_tiles + 3 - odd, g]]
        to_cross[:, g] = slab[:, ints[row_tiles + 2 + odd, g]]


def finish(scale, ints, parts, near, far, out, gram, inverse):
    me = lax.axis_index("help")
    volumes, steps, vectors, _ = gram.shape
    row_tiles, side = near.shape[2], near.shape[4]
    for q in range(inverse.shape[0]):
        inverse[ints[row_tiles + 1, q]] = q
    for j in range(row_tiles):
        slot = inverse[me * row_tiles + j]
        held = lax.rem(slot, row_tiles)
        step = lax.div(slot, row_tiles) ^ me
        pairs = [(near, 0), (near, 1), (far, 1), (far, 0)]
        block = near[0, :, held]
        for d, (ref, half) in enumerate(pairs):
            block = jnp.where(step == d, ref[half, :, held], block)
        out[:, :, j * side:(j + 1) * side] = block
    total = jnp.sum(parts[...].astype(jnp.float32), axis=0) * scale
    for step in range(steps):
        for v in range(volumes):
            at = (step * volumes + v) * vectors
            gram[v, step] = total[:, at:at + vectors]


def tile_pair(tiles, j, k):
    return jnp.concatenate(
        [jnp.concatenate([tiles[v, j, k], tiles[v, j, k + 1]], axis=1) for v in range(tiles.shape[0])],
        axis=0,
    )


def apply_first(ints, coefs, slab, pair, cross, tiles, first, gram, ext):
    volumes, row_tiles, slots, side, _ = tiles.shape
    slab_size = slab.shape[0]
    ghosts = pair.shape[0]
    vectors = slab.shape[1]
    me = lax.axis_index("help")
    odd = lax.rem(lax.axis_index("rows"), 2)
    ext[pl.ds(0, slab_size)] = slab[...]
    ext[pl.ds(slab_size + (1 - odd) * ghosts, ghosts)] = pair[...]
    ext[pl.ds(slab_size + odd * ghosts, ghosts)] = cross[...]
    for j in range(row_tiles):
        total = jnp.zeros((vectors, volumes * side), jnp.float32)
        for k in range(0, slots, 2):
            left = jnp.concatenate(
                [jnp.where(q < ints[row_tiles, j], ext[ints[j, q]], 0).astype(ext.dtype) for q in (k, k + 1)], axis=1
            )
            total += lax.dot_general(left, tile_pair(tiles, j, k), NT, preferred_element_type=jnp.float32)
        stored = slab[ints[row_tiles + 1, me * row_tiles + j]].astype(jnp.float32)
        for v in range(volumes):
            h = total[:, v * side:(v + 1) * side]
            first[v, j] = ((h - coefs[v] * stored) / coefs[volumes + v]).astype(first.dtype)
    for v in range(volumes):
        field = jnp.concatenate([first[v, j] for j in range(row_tiles)], axis=1)
        gram[v] = lax.dot_general(field, field, NT, preferred_element_type=jnp.float32)


def apply_second(
    ints, coefs, base, slab, pair, cross, tiles, first, gram_one, second, gram, ext
):
    volumes, row_tiles, slots, side, _ = tiles.shape
    slab_size = slab.shape[1]
    ghosts = pair.shape[1]
    vectors = slab.shape[2]
    me = lax.axis_index("help")
    odd = lax.rem(lax.axis_index("rows"), 2)
    ext[:, pl.ds(0, slab_size)] = slab[...]
    ext[:, pl.ds(slab_size + (1 - odd) * ghosts, ghosts)] = pair[...]
    ext[:, pl.ds(slab_size + odd * ghosts, ghosts)] = cross[...]
    for j in range(row_tiles):
        total = jnp.zeros((volumes * vectors, volumes * side), jnp.float32)
        for k in range(0, slots, 2):
            left = jnp.concatenate(
                [
                    jnp.concatenate(
                        [
                            jnp.where(q < ints[row_tiles, j], ext[v, ints[j, q]], 0).astype(ext.dtype)
                            for q in (k, k + 1)
                        ],
                        axis=1,
                    )
                    for v in range(volumes)
                ],
                axis=0,
            )
            total += lax.dot_general(left, tile_pair(tiles, j, k), NT, preferred_element_type=jnp.float32)
        stored = base[ints[row_tiles + 1, me * row_tiles + j]].astype(jnp.float32)
        for v in range(volumes):
            h = total[v * vectors:(v + 1) * vectors, v * side:(v + 1) * side]
            inner = h - coefs[v] * first[v, j].astype(jnp.float32)
            second[v, j] = (2.0 * inner / coefs[volumes + v] - stored).astype(second.dtype)
    parts = [gram_one[v] for v in range(volumes)]
    for v in range(volumes):
        field = jnp.concatenate([second[v, j] for j in range(row_tiles)], axis=1)
        parts.append(lax.dot_general(field, field, NT, preferred_element_type=jnp.float32))
    gram[...] = jnp.concatenate(parts, axis=1)


def summed_parts(value, groups):
    parts = jnp.broadcast_to(value.astype(jnp.bfloat16)[None], (len(groups[0]),) + value.shape)
    return lax.all_to_all(parts, ("rows", "help"), 0, 0, axis_index_groups=groups)


def per_device(panel, tiles, tile_cols, tile_count, row_assign, send_lists, centers, half_widths):
    helpers = lax.axis_size("help")
    rows = lax.axis_size("rows")
    volumes, row_tiles, slots, side, _ = tiles.shape
    vectors = panel.shape[0]
    ghosts = send_lists.shape[2]
    slab_size = row_tiles * helpers
    bf16 = panel.dtype
    depth = rows // (SIDE_CHIPS * CORES)

    def at(z, y, core, x):
        return ((z * SIDE_CHIPS + y) * CORES + core) * helpers + x

    def shape(*dims):
        return jax.ShapeDtypeStruct(dims, bf16)

    def gathered(shard):
        others = [
            lax.ppermute(shard, "help", [(i, i ^ d) for i in range(helpers)]) for d in range(1, helpers)
        ]
        return [shard] + others

    def exchanged(to_pair, to_cross):
        cross_pairs = [(s, (s + 1) % rows if s % 2 else (s - 1) % rows) for s in range(rows)]
        cross = lax.ppermute(to_cross, "rows", cross_pairs)
        pair = lax.ppermute(to_pair, "rows", [(s, s ^ 1) for s in range(rows)])
        return pair, cross

    params = pltpu.CompilerParams(vmem_limit_bytes=24 * 1024 * 1024)

    ints = jnp.concatenate(
        [
            jnp.pad(tile_cols, ((0, 0), (0, LANES - slots))),
            jnp.pad(tile_count[None], ((0, 0), (0, LANES - row_tiles))),
            jnp.pad(row_assign[None], ((0, 0), (0, LANES - slab_size))),
            jnp.pad(send_lists[0], ((0, 0), (0, LANES - ghosts))),
        ],
        axis=0,
    )
    coefs = jnp.concatenate([centers, half_widths])
    own_panel = pl.pallas_call(
        own_blocks,
        out_shape=shape(row_tiles, vectors, side),
        in_specs=[VMEM] * 2,
        out_specs=VMEM,
        compiler_params=params,
        name="own_blocks",
    )(panel, tiles)
    base, to_pair, to_cross = pl.pallas_call(
        functools.partial(spread_panel, helpers),
        out_shape=[shape(slab_size, vectors, side)] + [shape(ghosts, vectors, side)] * 2,
        in_specs=[SMEM] + [VMEM] * helpers,
        out_specs=[VMEM] * 3,
        compiler_params=params,
        name="spread_panel",
    )(ints, own_panel, *gathered(panel)[1:])
    pair, cross = exchanged(to_pair, to_cross)
    first, gram_one = pl.pallas_call(
        apply_first,
        out_shape=[
            shape(volumes, row_tiles, vectors, side),
            jax.ShapeDtypeStruct((volumes, vectors, vectors), jnp.float32),
        ],
        in_specs=[SMEM] * 2 + [VMEM] * 4,
        out_specs=[VMEM] * 2,
        scratch_shapes=[pltpu.VMEM((slab_size + 2 * ghosts, vectors, side), bf16)],
        compiler_params=params,
        name="apply_first",
    )(ints, coefs, base, pair, cross, tiles)
    slab, to_pair, to_cross = pl.pallas_call(
        functools.partial(spread_field, helpers),
        out_shape=[shape(volumes, slab_size, vectors, side)] + [shape(volumes, ghosts, vectors, side)] * 2,
        in_specs=[SMEM] + [VMEM] * helpers,
        out_specs=[VMEM] * 3,
        compiler_params=params,
        name="spread_field",
    )(ints, *gathered(first))
    pair, cross = exchanged(to_pair, to_cross)
    second, gram = pl.pallas_call(
        apply_second,
        out_shape=[
            shape(volumes, row_tiles, vectors, side),
            jax.ShapeDtypeStruct((vectors, 2 * volumes * vectors), jnp.float32),
        ],
        in_specs=[SMEM] * 2 + [VMEM] * 7,
        out_specs=[VMEM] * 2,
        scratch_shapes=[pltpu.VMEM((volumes, slab_size + 2 * ghosts, vectors, side), bf16)],
        compiler_params=params,
        name="apply_second",
    )(ints, coefs, base, slab, pair, cross, tiles, first, gram_one)

    near_pair = jnp.stack([second, lax.ppermute(second, "help", [(i, i ^ 1) for i in range(helpers)])])
    near = [
        [at(z, y, c, x) for y in range(SIDE_CHIPS) for x in range(helpers)]
        for z in range(depth)
        for c in range(CORES)
    ]
    far = [
        [at(z, y, c, x) for z in range(depth) for c in range(CORES)]
        for y in range(SIDE_CHIPS)
        for x in range(helpers)
    ]
    gram = jnp.sum(summed_parts(gram, near).astype(jnp.float32), axis=0)
    gram, near_pair = lax.optimization_barrier((gram, near_pair))
    far_pair = lax.ppermute(near_pair, "help", [(i, i ^ 3) for i in range(helpers)])
    parts = summed_parts(gram, far)
    filtered, gram = pl.pallas_call(
        functools.partial(finish, 1.0 / (row_tiles * side * helpers * rows)),
        out_shape=[
            shape(volumes, vectors, row_tiles * side),
            jax.ShapeDtypeStruct((volumes, 2, vectors, vectors), jnp.float32),
        ],
        in_specs=[SMEM] + [VMEM] * 3,
        out_specs=[VMEM] * 2,
        scratch_shapes=[pltpu.SMEM((slab_size,), jnp.int32)],
        compiler_params=params,
        name="finish",
    )(ints, parts, near_pair, far_pair)
    return filtered, gram


def solution(mesh):
    placed = (
        P(None, ("rows", "help")),
        P(None, ("rows", "help"), None, None, None),
        P(("rows", "help"), None),
        P(("rows", "help")),
        P("rows"),
        P("rows", None, None),
        P(),
        P(),
    )
    return jax.shard_map(
        per_device,
        mesh=mesh,
        in_specs=placed,
        out_specs=(P(None, None, ("rows", "help")), P()),
        check_vma=False,
    )
```

```python
import functools

import jax
import jax.numpy as jnp
from jax import lax
from jax.experimental import pallas as pl
from jax.experimental.pallas import tpu as pltpu
from jax.sharding import PartitionSpec as P

CORES = 2
LANES = 128
CHUNK = 8
SIDE_CHIPS = 4
NT = (((1,), (1,)), ((), ()))
VMEM = pl.BlockSpec(memory_space=pltpu.VMEM)
SMEM = pl.BlockSpec(memory_space=pltpu.SMEM)


def own_blocks(panel, tiles, blocks):
    side = blocks.shape[2]
    for j in range(blocks.shape[0]):
        blocks[j] = panel[:, j * side:(j + 1) * side]


def spread_panel(helpers, ints, *refs):
    shards, (slab, to_pair, to_cross) = refs[:helpers], refs[helpers:]
    me = lax.axis_index("help")
    odd = lax.rem(lax.axis_index("rows"), 2)
    side = slab.shape[2]
    row_tiles = slab.shape[0] // helpers
    for d in range(helpers):
        base = (me ^ d) * row_tiles
        for j in range(row_tiles):
            slab[base + j] = shards[d][:, j * side:(j + 1) * side] if d else shards[0][j]
    for g in range(to_pair.shape[0]):
        to_pair[g] = slab[ints[row_tiles + 3 - odd, g]]
        to_cross[g] = slab[ints[row_tiles + 2 + odd, g]]


def spread_field(helpers, ints, *refs):
    shards, (slab, to_pair, to_cross) = refs[:helpers], refs[helpers:]
    me = lax.axis_index("help")
    odd = lax.rem(lax.axis_index("rows"), 2)
    row_tiles = slab.shape[1] // helpers
    for d in range(helpers):
        base = (me ^ d) * row_tiles
        for j in range(row_tiles):
            slab[:, ints[row_tiles + 1, base + j]] = shards[d][:, j]
    for g in range(to_pair.shape[1]):
        to_pair[:, g] = slab[:, ints[row_tiles + 3 - odd, g]]
        to_cross[:, g] = slab[:, ints[row_tiles + 2 + odd, g]]


def finish(scale, ints, parts, near, far, out, gram, inverse):
    me = lax.axis_index("help")
    volumes, steps, vectors, _ = gram.shape
    row_tiles, side = near.shape[2], near.shape[4]
    for q in range(inverse.shape[0]):
        inverse[ints[row_tiles + 1, q]] = q
    for j in range(row_tiles):
        slot = inverse[me * row_tiles + j]
        held = lax.rem(slot, row_tiles)
        step = lax.div(slot, row_tiles) ^ me
        pairs = [(near, 0), (near, 1), (far, 1), (far, 0)]
        block = near[0, :, held]
        for d, (ref, half) in enumerate(pairs):
            block = jnp.where(step == d, ref[half, :, held], block)
        out[:, :, j * side:(j + 1) * side] = block
    total = jnp.sum(parts[...].astype(jnp.float32), axis=0) * scale
    for step in range(steps):
        for v in range(volumes):
            at = (step * volumes + v) * vectors
            gram[v, step] = total[:, at:at + vectors]


def tile_pair(tiles, j, k):
    return jnp.concatenate(
        [jnp.concatenate([tiles[v, j, k], tiles[v, j, k + 1]], axis=1) for v in range(tiles.shape[0])],
        axis=0,
    )


def list_cross(ints, listed, row_tiles, slots, slab_size, ghosts, odd):
    found = jnp.int32(0)
    for j in range(row_tiles):
        for k in range(slots):
            col = ints[j, k]
            side = jnp.where(col >= slab_size + ghosts, 1, 0)
            crosses = jnp.logical_and(col >= slab_size, side == odd)
            listed[found] = j * slots + k
            found += jnp.where(jnp.logical_and(crosses, k < ints[row_tiles, j]), 1, 0)
    listed[row_tiles * slots + 1] = found


def near_block(ints, ext, j, k, slab_size, ghosts, row_tiles, odd, lead):
    col = ints[j, k]
    side = jnp.where(col >= slab_size + ghosts, 1, 0)
    near = jnp.logical_or(col < slab_size, side != odd)
    used = jnp.logical_and(near, k < ints[row_tiles, j])
    return jnp.where(used, ext[lead + (col,)], 0).astype(ext.dtype)


def near_first(ints, slab, pair, tiles, part, listed, ext):
    volumes, row_tiles, slots, side, _ = tiles.shape
    slab_size, ghosts, vectors = slab.shape[0], pair.shape[0], slab.shape[1]
    odd = lax.rem(lax.axis_index("rows"), 2)
    ext[pl.ds(0, slab_size)] = slab[...]
    ext[pl.ds(slab_size + (1 - odd) * ghosts, ghosts)] = pair[...]
    for j in range(row_tiles):
        total = jnp.zeros((vectors, volumes * side), jnp.float32)
        for k in range(0, slots, 2):
            left = jnp.concatenate(
                [near_block(ints, ext, j, q, slab_size, ghosts, row_tiles, odd, ()) for q in (k, k + 1)], axis=1
            )
            total += lax.dot_general(left, tile_pair(tiles, j, k), NT, preferred_element_type=jnp.float32)
        for v in range(volumes):
            part[v, j] = total[:, v * side:(v + 1) * side]
    list_cross(ints, listed, row_tiles, slots, slab_size, ghosts, odd)


def near_second(ints, slab, pair, tiles, part, ext):
    volumes, row_tiles, slots, side, _ = tiles.shape
    slab_size, ghosts, vectors = slab.shape[1], pair.shape[1], slab.shape[2]
    odd = lax.rem(lax.axis_index("rows"), 2)
    ext[:, pl.ds(0, slab_size)] = slab[...]
    ext[:, pl.ds(slab_size + (1 - odd) * ghosts, ghosts)] = pair[...]
    for j in range(row_tiles):
        total = jnp.zeros((volumes * vectors, volumes * side), jnp.float32)
        for k in range(0, slots, 2):
            left = jnp.concatenate(
                [
                    jnp.concatenate(
                        [
                            near_block(ints, ext, j, q, slab_size, ghosts, row_tiles, odd, (v,))
                            for q in (k, k + 1)
                        ],
                        axis=1,
                    )
                    for v in range(volumes)
                ],
                axis=0,
            )
            total += lax.dot_general(left, tile_pair(tiles, j, k), NT, preferred_element_type=jnp.float32)
        for v in range(volumes):
            part[v, j] = total[v * vectors:(v + 1) * vectors, v * side:(v + 1) * side]


def add_cross(ints, listed, cross, tiles, acc, lead):
    volumes, row_tiles, slots, side, _ = tiles.shape
    ghosts = cross.shape[len(lead)]
    helpers = lax.axis_size("help")
    odd = lax.rem(lax.axis_index("rows"), 2)
    start = row_tiles * helpers + odd * ghosts
    found = listed[row_tiles * slots + 1]

    def chunk(i, carry):
        products = []
        for u in range(CHUNK):
            at = i * CHUNK + u
            used = at < found
            item = jnp.where(used, listed[at], 0)
            j = lax.div(item, slots)
            k = lax.rem(item, slots)
            g = jnp.where(used, ints[j, k] - start, 0)
            if lead:
                blocks = jnp.concatenate([cross[v, g] for v in range(volumes)], axis=0)
            else:
                blocks = cross[g]
            blocks = jnp.where(used, blocks, 0).astype(cross.dtype)
            weights = jnp.concatenate([tiles[v, j, k] for v in range(volumes)], axis=0)
            products.append((j, lax.dot_general(blocks, weights, NT, preferred_element_type=jnp.float32)))
        for j, product in products:
            for v in range(volumes):
                rows = product.shape[0] // volumes if lead else product.shape[0]
                low = v * rows if lead else 0
                acc[v, j] += product[low:low + rows, v * side:(v + 1) * side]
        return carry

    lax.fori_loop(0, lax.div(found + CHUNK - 1, CHUNK), chunk, 0)


def apply_first(ints, coefs, listed, slab, cross, tiles, part, first, gram, acc):
    volumes, row_tiles = first.shape[:2]
    me = lax.axis_index("help")
    acc[...] = part[...]
    scales = [1.0 / jnp.full(acc.shape[2:], coefs[volumes + v]) for v in range(volumes)]
    add_cross(ints, listed, cross, tiles, acc, ())
    for j in range(row_tiles):
        stored = slab[ints[row_tiles + 1, me * row_tiles + j]].astype(jnp.float32)
        for v in range(volumes):
            first[v, j] = ((acc[v, j] - coefs[v] * stored) * scales[v]).astype(first.dtype)
    for v in range(volumes):
        field = jnp.concatenate([first[v, j] for j in range(row_tiles)], axis=1)
        gram[v] = lax.dot_general(field, field, NT, preferred_element_type=jnp.float32)


def apply_second(ints, coefs, listed, base, cross, tiles, part, first, gram_one, second, gram, acc):
    volumes, row_tiles = first.shape[:2]
    me = lax.axis_index("help")
    acc[...] = part[...]
    scales = [1.0 / jnp.full(acc.shape[2:], coefs[volumes + v]) for v in range(volumes)]
    add_cross(ints, listed, cross, tiles, acc, (0,))
    for j in range(row_tiles):
        stored = base[ints[row_tiles + 1, me * row_tiles + j]].astype(jnp.float32)
        for v in range(volumes):
            inner = acc[v, j] - coefs[v] * first[v, j].astype(jnp.float32)
            second[v, j] = (2.0 * inner * scales[v] - stored).astype(second.dtype)
    parts = [gram_one[v] for v in range(volumes)]
    for v in range(volumes):
        field = jnp.concatenate([second[v, j] for j in range(row_tiles)], axis=1)
        parts.append(lax.dot_general(field, field, NT, preferred_element_type=jnp.float32))
    gram[...] = jnp.concatenate(parts, axis=1)


def summed_parts(value, groups):
    parts = jnp.broadcast_to(value.astype(jnp.bfloat16)[None], (len(groups[0]),) + value.shape)
    return lax.all_to_all(parts, ("rows", "help"), 0, 0, axis_index_groups=groups)


def per_device(panel, tiles, tile_cols, tile_count, row_assign, send_lists, centers, half_widths):
    helpers = lax.axis_size("help")
    rows = lax.axis_size("rows")
    volumes, row_tiles, slots, side, _ = tiles.shape
    vectors = panel.shape[0]
    ghosts = send_lists.shape[2]
    slab_size = row_tiles * helpers
    bf16 = panel.dtype
    depth = rows // (SIDE_CHIPS * CORES)

    def at(z, y, core, x):
        return ((z * SIDE_CHIPS + y) * CORES + core) * helpers + x

    def shape(*dims):
        return jax.ShapeDtypeStruct(dims, bf16)

    def gathered(shard):
        others = [
            lax.ppermute(shard, "help", [(i, i ^ d) for i in range(helpers)]) for d in range(1, helpers)
        ]
        return [shard] + others

    def exchanged(to_pair, to_cross):
        cross_pairs = [(s, (s + 1) % rows if s % 2 else (s - 1) % rows) for s in range(rows)]
        cross = lax.ppermute(to_cross, "rows", cross_pairs)
        pair = lax.ppermute(to_pair, "rows", [(s, s ^ 1) for s in range(rows)])
        return pair, cross

    params = pltpu.CompilerParams(vmem_limit_bytes=24 * 1024 * 1024)

    ints = jnp.concatenate(
        [
            jnp.pad(tile_cols, ((0, 0), (0, LANES - slots))),
            jnp.pad(tile_count[None], ((0, 0), (0, LANES - row_tiles))),
            jnp.pad(row_assign[None], ((0, 0), (0, LANES - slab_size))),
            jnp.pad(send_lists[0], ((0, 0), (0, LANES - ghosts))),
        ],
        axis=0,
    )
    coefs = jnp.concatenate([centers, half_widths])
    own_panel = pl.pallas_call(
        own_blocks,
        out_shape=shape(row_tiles, vectors, side),
        in_specs=[VMEM] * 2,
        out_specs=VMEM,
        compiler_params=params,
        name="own_blocks",
    )(panel, tiles)
    base, to_pair, to_cross = pl.pallas_call(
        functools.partial(spread_panel, helpers),
        out_shape=[shape(slab_size, vectors, side)] + [shape(ghosts, vectors, side)] * 2,
        in_specs=[SMEM] + [VMEM] * helpers,
        out_specs=[VMEM] * 3,
        compiler_params=params,
        name="spread_panel",
    )(ints, own_panel, *gathered(panel)[1:])
    pair, cross = exchanged(to_pair, to_cross)
    part_shape = jax.ShapeDtypeStruct((volumes, row_tiles, vectors, side), jnp.float32)
    listed_size = row_tiles * slots + 2
    product_cost = pl.CostEstimate(
        flops=4 * volumes * row_tiles * slots * side * side * vectors,
        bytes_accessed=2 * tiles.size,
        transcendentals=0,
    )
    part, listed = pl.pallas_call(
        near_first,
        out_shape=[part_shape, jax.ShapeDtypeStruct((listed_size,), jnp.int32)],
        in_specs=[SMEM] + [VMEM] * 3,
        out_specs=[VMEM, SMEM],
        scratch_shapes=[pltpu.VMEM((slab_size + 2 * ghosts, vectors, side), bf16)],
        compiler_params=params,
        cost_estimate=product_cost,
        name="near_first",
    )(ints, base, pair, tiles)
    first, gram_one = pl.pallas_call(
        apply_first,
        out_shape=[
            shape(volumes, row_tiles, vectors, side),
            jax.ShapeDtypeStruct((volumes, vectors, vectors), jnp.float32),
        ],
        in_specs=[SMEM] * 3 + [VMEM] * 4,
        out_specs=[VMEM] * 2,
        scratch_shapes=[pltpu.VMEM(part_shape.shape, jnp.float32)],
        compiler_params=params,
        name="apply_first",
    )(ints, coefs, listed, base, cross, tiles, part)
    slab, to_pair, to_cross = pl.pallas_call(
        functools.partial(spread_field, helpers),
        out_shape=[shape(volumes, slab_size, vectors, side)] + [shape(volumes, ghosts, vectors, side)] * 2,
        in_specs=[SMEM] + [VMEM] * helpers,
        out_specs=[VMEM] * 3,
        compiler_params=params,
        name="spread_field",
    )(ints, *gathered(first))
    pair, cross = exchanged(to_pair, to_cross)
    part = pl.pallas_call(
        near_second,
        out_shape=part_shape,
        in_specs=[SMEM] + [VMEM] * 3,
        out_specs=VMEM,
        scratch_shapes=[pltpu.VMEM((volumes, slab_size + 2 * ghosts, vectors, side), bf16)],
        compiler_params=params,
        cost_estimate=product_cost,
        name="near_second",
    )(ints, slab, pair, tiles)
    second, gram = pl.pallas_call(
        apply_second,
        out_shape=[
            shape(volumes, row_tiles, vectors, side),
            jax.ShapeDtypeStruct((vectors, 2 * volumes * vectors), jnp.float32),
        ],
        in_specs=[SMEM] * 3 + [VMEM] * 6,
        out_specs=[VMEM] * 2,
        scratch_shapes=[pltpu.VMEM(part_shape.shape, jnp.float32)],
        compiler_params=params,
        name="apply_second",
    )(ints, coefs, listed, base, cross, tiles, part, first, gram_one)

    near_pair = jnp.stack([second, lax.ppermute(second, "help", [(i, i ^ 1) for i in range(helpers)])])
    near = [
        [at(z, y, c, x) for y in range(SIDE_CHIPS) for x in range(helpers)]
        for z in range(depth)
        for c in range(CORES)
    ]
    far = [
        [at(z, y, c, x) for z in range(depth) for c in range(CORES)]
        for y in range(SIDE_CHIPS)
        for x in range(helpers)
    ]
    gram = jnp.sum(summed_parts(gram, near).astype(jnp.float32), axis=0)
    gram, near_pair = lax.optimization_barrier((gram, near_pair))
    far_pair = lax.ppermute(near_pair, "help", [(i, i ^ 3) for i in range(helpers)])
    parts = summed_parts(gram, far)
    filtered, gram = pl.pallas_call(
        functools.partial(finish, 1.0 / (row_tiles * side * helpers * rows)),
        out_shape=[
            shape(volumes, vectors, row_tiles * side),
            jax.ShapeDtypeStruct((volumes, 2, vectors, vectors), jnp.float32),
        ],
        in_specs=[SMEM] + [VMEM] * 3,
        out_specs=[VMEM] * 2,
        scratch_shapes=[pltpu.SMEM((slab_size,), jnp.int32)],
        compiler_params=params,
        name="finish",
    )(ints, parts, near_pair, far_pair)
    return filtered, gram


def solution(mesh):
    placed = (
        P(None, ("rows", "help")),
        P(None, ("rows", "help"), None, None, None),
        P(("rows", "help"), None),
        P(("rows", "help")),
        P("rows"),
        P("rows", None, None),
        P(),
        P(),
    )
    return jax.shard_map(
        per_device,
        mesh=mesh,
        in_specs=placed,
        out_specs=(P(None, None, ("rows", "help")), P()),
        check_vma=False,
    )
```

```python
import functools

import jax
import jax.numpy as jnp
from jax import lax
from jax.experimental import pallas as pl
from jax.experimental.pallas import tpu as pltpu
from jax.sharding import PartitionSpec as P

CORES = 2
LANES = 128
CHUNK = 8
SIDE_CHIPS = 4
NT = (((1,), (1,)), ((), ()))
VMEM = pl.BlockSpec(memory_space=pltpu.VMEM)


def own_blocks(panel, tiles, blocks):
    side = blocks.shape[2]
    for j in range(blocks.shape[0]):
        blocks[j] = panel[:, j * side:(j + 1) * side]


def rolled(row, first):
    return pltpu.roll(row, lax.rem(row.shape[1] - first, row.shape[1]), 1)


def ghost_rows(ints, row_tiles, odd):
    to_prev = ints[row_tiles + 2:row_tiles + 3, :]
    to_next = ints[row_tiles + 3:row_tiles + 4, :]
    return jnp.where(odd == 1, to_prev, to_next), jnp.where(odd == 1, to_next, to_prev)


def spread_panel(helpers, ints, *refs):
    shards, (slab, to_pair, to_cross) = refs[:helpers], refs[helpers:]
    me = lax.axis_index("help")
    odd = lax.rem(lax.axis_index("rows"), 2)
    side = slab.shape[2]
    row_tiles = slab.shape[0] // helpers
    for d in range(helpers):
        base = (me ^ d) * row_tiles
        for j in range(row_tiles):
            slab[base + j] = shards[d][:, j * side:(j + 1) * side] if d else shards[0][j]
    pair_rows, cross_rows = ghost_rows(ints, row_tiles, odd)
    for g in range(to_pair.shape[0]):
        to_cross[g] = slab[cross_rows[0, g]]
        to_pair[g] = slab[pair_rows[0, g]]


def spread_field(helpers, table, *refs):
    shards, (slab, to_pair, to_cross) = refs[:helpers], refs[helpers:]
    me = lax.axis_index("help")
    row_tiles = slab.shape[1] // helpers
    for d in range(helpers):
        slab[:, pl.ds((me ^ d) * row_tiles, row_tiles)] = shards[d][...]
    for g in range(to_pair.shape[1]):
        to_cross[:, g] = slab[:, table[3, g]]
        to_pair[:, g] = slab[:, table[2, g]]


def place_field(helpers, table, *refs):
    shards, out = refs[:helpers], refs[helpers]
    me = lax.axis_index("help")
    row_tiles, side = shards[0].shape[1], shards[0].shape[3]
    slots = rolled(table[4:5, :], me * row_tiles)
    for j in range(row_tiles):
        slot = slots[0, j]
        held = lax.rem(slot, row_tiles)
        step = lax.div(slot, row_tiles) ^ me
        block = shards[0][:, held]
        for d in range(1, helpers):
            block = jnp.where(step == d, shards[d][:, held], block)
        out[:, :, j * side:(j + 1) * side] = block


def finish_gram(scale, parts, gram):
    volumes, steps, vectors, _ = gram.shape
    total = jnp.sum(parts[...].astype(jnp.float32), axis=0) * scale
    for step in range(steps):
        for v in range(volumes):
            at = (step * volumes + v) * vectors
            gram[v, step] = total[:, at:at + vectors]


def tile_pair(tiles, j, k):
    return jnp.concatenate(
        [jnp.concatenate([tiles[v, j, k], tiles[v, j, k + 1]], axis=1) for v in range(tiles.shape[0])],
        axis=0,
    )


def near_block(ints, ext, j, k, slab_size, ghosts, row_tiles, odd, lead):
    col = ints[j, k]
    side = jnp.where(col >= slab_size + ghosts, 1, 0)
    near = jnp.logical_or(col < slab_size, side != odd)
    used = jnp.logical_and(near, k < ints[row_tiles, j])
    return jnp.where(used, ext[lead + (col,)], 0).astype(ext.dtype)


def make_table(ints, built, row_tiles, slots, slab_size, ghosts, odd):
    low = slab_size + odd * ghosts
    found = jnp.int32(0)
    for j in range(row_tiles):
        live = ints[row_tiles, j]
        for k in range(slots):
            ghost = ints[j, k] - low
            built[0, found] = (j * slots + k) * ghosts + ghost
            crosses = jnp.logical_and(jnp.logical_and(ghost >= 0, ghost < ghosts), k < live)
            found += jnp.where(crosses, 1, 0)
    built[1, 0] = found
    for q in range(slab_size):
        built[4, ints[row_tiles + 1, q]] = q
    pair_rows, cross_rows = ghost_rows(ints, row_tiles, odd)
    for g in range(ghosts):
        built[2, g] = built[4, pair_rows[0, g]]
        built[3, g] = built[4, cross_rows[0, g]]


def near_first(ints, slab, pair, tiles, part, stored, table, ext, built, done):
    volumes, row_tiles, slots, side, _ = tiles.shape
    slab_size, ghosts, vectors = slab.shape[0], pair.shape[0], slab.shape[1]
    me = lax.axis_index("help")
    odd = lax.rem(lax.axis_index("rows"), 2)
    make_table(ints, built, row_tiles, slots, slab_size, ghosts, odd)
    hand_over = pltpu.make_async_copy(built, table, done)
    hand_over.start()
    ext[pl.ds(0, slab_size)] = slab[...]
    ext[pl.ds(slab_size + (1 - odd) * ghosts, ghosts)] = pair[...]
    mine = rolled(ints[row_tiles + 1:row_tiles + 2, :], me * row_tiles)
    for j in range(row_tiles):
        total = jnp.zeros((vectors, volumes * side), jnp.float32)
        for k in range(0, slots, 2):
            left = jnp.concatenate(
                [near_block(ints, ext, j, q, slab_size, ghosts, row_tiles, odd, ()) for q in (k, k + 1)], axis=1
            )
            total += lax.dot_general(left, tile_pair(tiles, j, k), NT, preferred_element_type=jnp.float32)
        for v in range(volumes):
            part[v, j] = total[:, v * side:(v + 1) * side]
        stored[j] = slab[mine[0, j]]
    hand_over.wait()


def near_second(ints, slab, pair, tiles, part, ext):
    volumes, row_tiles, slots, side, _ = tiles.shape
    slab_size, ghosts, vectors = slab.shape[1], pair.shape[1], slab.shape[2]
    odd = lax.rem(lax.axis_index("rows"), 2)
    for q in range(slab_size):
        ext[:, ints[row_tiles + 1, q]] = slab[:, q]
    ext[:, pl.ds(slab_size + (1 - odd) * ghosts, ghosts)] = pair[...]
    for j in range(row_tiles):
        total = jnp.zeros((volumes * vectors, volumes * side), jnp.float32)
        for k in range(0, slots, 2):
            left = jnp.concatenate(
                [
                    jnp.concatenate(
                        [
                            near_block(ints, ext, j, q, slab_size, ghosts, row_tiles, odd, (v,))
                            for q in (k, k + 1)
                        ],
                        axis=1,
                    )
                    for v in range(volumes)
                ],
                axis=0,
            )
            total += lax.dot_general(left, tile_pair(tiles, j, k), NT, preferred_element_type=jnp.float32)
        for v in range(volumes):
            part[v, j] = total[v * vectors:(v + 1) * vectors, v * side:(v + 1) * side]


def add_cross(table, cross, tiles, acc, lead):
    volumes, row_tiles, slots, side, _ = tiles.shape
    ghosts = cross.shape[len(lead)]
    items = table[0:1, :]
    found = table[1, 0]

    def chunk_items(i):
        row = rolled(items, lax.rem(i * CHUNK, LANES))
        return tuple(row[0, u] for u in range(CHUNK))

    def chunk(i, held):
        products = []
        for u in range(CHUNK):
            used = i * CHUNK + u < found
            item = jnp.where(used, held[u], 0)
            tile = lax.div(item, ghosts)
            g = lax.rem(item, ghosts)
            j = lax.div(tile, slots)
            k = lax.rem(tile, slots)
            if lead:
                blocks = jnp.concatenate([cross[v, g] for v in range(volumes)], axis=0)
            else:
                blocks = cross[g]
            blocks = jnp.where(used, blocks, 0).astype(cross.dtype)
            weights = jnp.concatenate([tiles[v, j, k] for v in range(volumes)], axis=0)
            products.append((j, lax.dot_general(blocks, weights, NT, preferred_element_type=jnp.float32)))
        following = chunk_items(i + 1)
        for j, product in products:
            for v in range(volumes):
                rows = product.shape[0] // volumes if lead else product.shape[0]
                low = v * rows if lead else 0
                acc[v, j] += product[low:low + rows, v * side:(v + 1) * side]
        return following

    lax.fori_loop(0, lax.div(found + CHUNK - 1, CHUNK), chunk, chunk_items(jnp.int32(0)))


def apply_first(coefs, table, stored, cross, tiles, part, first, gram, acc):
    volumes, row_tiles = first.shape[:2]
    acc[...] = part[...]
    add_cross(table, cross, tiles, acc, ())
    for v in range(volumes):
        centre = coefs[v:v + 1, :]
        scale = 1.0 / coefs[volumes + v:volumes + v + 1, :]
        for j in range(row_tiles):
            first[v, j] = ((acc[v, j] - centre * stored[j].astype(jnp.float32)) * scale).astype(first.dtype)
        field = jnp.concatenate([first[v, j] for j in range(row_tiles)], axis=1)
        gram[v] = lax.dot_general(field, field, NT, preferred_element_type=jnp.float32)


def apply_second(coefs, table, stored, cross, tiles, part, first, gram_one, second, gram, acc):
    volumes, row_tiles = first.shape[:2]
    acc[...] = part[...]
    add_cross(table, cross, tiles, acc, (0,))
    parts = [gram_one[v] for v in range(volumes)]
    for v in range(volumes):
        centre = coefs[v:v + 1, :]
        scale = 2.0 / coefs[volumes + v:volumes + v + 1, :]
        for j in range(row_tiles):
            inner = acc[v, j] - centre * first[v, j].astype(jnp.float32)
            second[v, j] = (inner * scale - stored[j].astype(jnp.float32)).astype(second.dtype)
        field = jnp.concatenate([second[v, j] for j in range(row_tiles)], axis=1)
        parts.append(lax.dot_general(field, field, NT, preferred_element_type=jnp.float32))
    gram[...] = jnp.concatenate(parts, axis=1)


def summed_parts(value, groups):
    parts = jnp.broadcast_to(value.astype(jnp.bfloat16)[None], (len(groups[0]),) + value.shape)
    return lax.all_to_all(parts, ("rows", "help"), 0, 0, axis_index_groups=groups)


def per_device(panel, tiles, tile_cols, tile_count, row_assign, send_lists, centers, half_widths):
    helpers = lax.axis_size("help")
    rows = lax.axis_size("rows")
    volumes, row_tiles, slots, side, _ = tiles.shape
    vectors = panel.shape[0]
    ghosts = send_lists.shape[2]
    slab_size = row_tiles * helpers
    bf16 = panel.dtype
    depth = rows // (SIDE_CHIPS * CORES)

    def at(z, y, core, x):
        return ((z * SIDE_CHIPS + y) * CORES + core) * helpers + x

    def shape(*dims):
        return jax.ShapeDtypeStruct(dims, bf16)

    def gathered(shard):
        others = [
            lax.ppermute(shard, "help", [(i, i ^ d) for i in range(helpers)]) for d in range(1, helpers)
        ]
        return [shard] + others

    def exchanged(to_pair, to_cross):
        cross_pairs = [(s, (s + 1) % rows if s % 2 else (s - 1) % rows) for s in range(rows)]
        cross = lax.ppermute(to_cross, "rows", cross_pairs)
        pair = lax.ppermute(to_pair, "rows", [(s, s ^ 1) for s in range(rows)])
        return pair, cross

    params = pltpu.CompilerParams(vmem_limit_bytes=24 * 1024 * 1024)

    ints = jnp.concatenate(
        [
            jnp.pad(tile_cols, ((0, 0), (0, LANES - slots))),
            jnp.pad(tile_count[None], ((0, 0), (0, LANES - row_tiles))),
            jnp.pad(row_assign[None], ((0, 0), (0, LANES - slab_size))),
            jnp.pad(send_lists[0], ((0, 0), (0, LANES - ghosts))),
        ],
        axis=0,
    )
    coefs = jnp.broadcast_to(jnp.concatenate([centers, half_widths])[:, None], (2 * volumes, LANES))
    own_panel = pl.pallas_call(
        own_blocks,
        out_shape=shape(row_tiles, vectors, side),
        in_specs=[VMEM] * 2,
        out_specs=VMEM,
        compiler_params=params,
        name="own_blocks",
    )(panel, tiles)
    base, to_pair, to_cross = pl.pallas_call(
        functools.partial(spread_panel, helpers),
        out_shape=[shape(slab_size, vectors, side)] + [shape(ghosts, vectors, side)] * 2,
        in_specs=[VMEM] * (1 + helpers),
        out_specs=[VMEM] * 3,
        compiler_params=params,
        name="spread_panel",
    )(ints, own_panel, *gathered(panel)[1:])
    pair, cross = exchanged(to_pair, to_cross)
    part_shape = jax.ShapeDtypeStruct((volumes, row_tiles, vectors, side), jnp.float32)
    product_cost = pl.CostEstimate(
        flops=4 * volumes * row_tiles * slots * side * side * vectors,
        bytes_accessed=2 * tiles.size,
        transcendentals=0,
    )
    table_shape = (5, LANES)
    part, stored, table = pl.pallas_call(
        near_first,
        out_shape=[
            part_shape,
            shape(row_tiles, vectors, side),
            jax.ShapeDtypeStruct(table_shape, jnp.int32),
        ],
        in_specs=[VMEM] * 4,
        out_specs=[VMEM] * 3,
        scratch_shapes=[
            pltpu.VMEM((slab_size + 2 * ghosts, vectors, side), bf16),
            pltpu.SMEM(table_shape, jnp.int32),
            pltpu.SemaphoreType.DMA,
        ],
        compiler_params=params,
        cost_estimate=product_cost,
        name="near_first",
    )(ints, base, pair, tiles)
    first, gram_one = pl.pallas_call(
        apply_first,
        out_shape=[
            shape(volumes, row_tiles, vectors, side),
            jax.ShapeDtypeStruct((volumes, vectors, vectors), jnp.float32),
        ],
        in_specs=[VMEM] * 6,
        out_specs=[VMEM] * 2,
        scratch_shapes=[pltpu.VMEM(part_shape.shape, jnp.float32)],
        compiler_params=params,
        name="apply_first",
    )(coefs, table, stored, cross, tiles, part)
    slab, to_pair, to_cross = pl.pallas_call(
        functools.partial(spread_field, helpers),
        out_shape=[shape(volumes, slab_size, vectors, side)] + [shape(volumes, ghosts, vectors, side)] * 2,
        in_specs=[VMEM] * (1 + helpers),
        out_specs=[VMEM] * 3,
        compiler_params=params,
        name="spread_field",
    )(table, *gathered(first))
    pair, cross = exchanged(to_pair, to_cross)
    part = pl.pallas_call(
        near_second,
        out_shape=part_shape,
        in_specs=[VMEM] * 4,
        out_specs=VMEM,
        scratch_shapes=[pltpu.VMEM((volumes, slab_size + 2 * ghosts, vectors, side), bf16)],
        compiler_params=params,
        cost_estimate=product_cost,
        name="near_second",
    )(ints, slab, pair, tiles)
    second, gram = pl.pallas_call(
        apply_second,
        out_shape=[
            shape(volumes, row_tiles, vectors, side),
            jax.ShapeDtypeStruct((vectors, 2 * volumes * vectors), jnp.float32),
        ],
        in_specs=[VMEM] * 8,
        out_specs=[VMEM] * 2,
        scratch_shapes=[pltpu.VMEM(part_shape.shape, jnp.float32)],
        compiler_params=params,
        name="apply_second",
    )(coefs, table, stored, cross, tiles, part, first, gram_one)

    shards = gathered(second)
    near = [
        [at(z, y, c, x) for y in range(SIDE_CHIPS) for x in range(helpers)]
        for z in range(depth)
        for c in range(CORES)
    ]
    far = [
        [at(z, y, c, x) for z in range(depth) for c in range(CORES)]
        for y in range(SIDE_CHIPS)
        for x in range(helpers)
    ]
    gram = jnp.sum(summed_parts(gram, near).astype(jnp.float32), axis=0)
    gram, shards[1], shards[3] = lax.optimization_barrier((gram, shards[1], shards[3]))
    parts = summed_parts(gram, far)
    filtered = pl.pallas_call(
        functools.partial(place_field, helpers),
        out_shape=shape(volumes, vectors, row_tiles * side),
        in_specs=[VMEM] * (1 + helpers),
        out_specs=VMEM,
        compiler_params=params,
        name="place_field",
    )(table, *shards)
    gram = pl.pallas_call(
        functools.partial(finish_gram, 1.0 / (row_tiles * side * helpers * rows)),
        out_shape=jax.ShapeDtypeStruct((volumes, 2, vectors, vectors), jnp.float32),
        in_specs=[VMEM],
        out_specs=VMEM,
        compiler_params=params,
        name="finish_gram",
    )(parts)
    return filtered, gram


def solution(mesh):
    placed = (
        P(None, ("rows", "help")),
        P(None, ("rows", "help"), None, None, None),
        P(("rows", "help"), None),
        P(("rows", "help")),
        P("rows"),
        P("rows", None, None),
        P(),
        P(),
    )
    return jax.shard_map(
        per_device,
        mesh=mesh,
        in_specs=placed,
        out_specs=(P(None, None, ("rows", "help")), P()),
        check_vma=False,
    )
```

```python
import functools

import jax
import jax.numpy as jnp
from jax import lax
from jax.experimental import pallas as pl
from jax.experimental.pallas import tpu as pltpu
from jax.sharding import PartitionSpec as P

CORES = 2
LANES = 128
CHUNK = 8
SIDE_CHIPS = 4
NT = (((1,), (1,)), ((), ()))
VMEM = pl.BlockSpec(memory_space=pltpu.VMEM)


def own_blocks(panel, tiles, blocks):
    side = blocks.shape[2]
    for j in range(blocks.shape[0]):
        blocks[j] = panel[:, j * side:(j + 1) * side]


def rolled(row, first):
    return pltpu.roll(row, lax.rem(row.shape[1] - first, row.shape[1]), 1)


def ghost_rows(ints, row_tiles, odd):
    to_prev = ints[row_tiles + 2:row_tiles + 3, :]
    to_next = ints[row_tiles + 3:row_tiles + 4, :]
    return jnp.where(odd == 1, to_prev, to_next), jnp.where(odd == 1, to_next, to_prev)


def spread_panel(helpers, ints, *refs):
    shards, (slab, to_pair, to_cross) = refs[:helpers], refs[helpers:]
    me = lax.axis_index("help")
    odd = lax.rem(lax.axis_index("rows"), 2)
    side = slab.shape[2]
    row_tiles = slab.shape[0] // helpers
    for d in range(helpers):
        base = (me ^ d) * row_tiles
        for j in range(row_tiles):
            slab[base + j] = shards[d][:, j * side:(j + 1) * side] if d else shards[0][j]
    pair_rows, cross_rows = ghost_rows(ints, row_tiles, odd)
    for g in range(to_pair.shape[0]):
        to_cross[g] = slab[cross_rows[0, g]]
        to_pair[g] = slab[pair_rows[0, g]]


def spread_field(helpers, table, *refs):
    shards, (slab, to_pair, to_cross) = refs[:helpers], refs[helpers:]
    me = lax.axis_index("help")
    row_tiles = slab.shape[1] // helpers
    for d in range(helpers):
        slab[:, pl.ds((me ^ d) * row_tiles, row_tiles)] = shards[d][...]
    for g in range(to_pair.shape[1]):
        to_cross[:, g] = slab[:, table[3, g]]
        to_pair[:, g] = slab[:, table[2, g]]


def finish(helpers, scale, table, parts, *refs):
    shards, (out, gram) = refs[:helpers], refs[helpers:]
    me = lax.axis_index("help")
    row_tiles, side = shards[0].shape[1], shards[0].shape[3]
    slots = rolled(table[4:5, :], me * row_tiles)
    for j in range(row_tiles):
        slot = slots[0, j]
        held = lax.rem(slot, row_tiles)
        step = lax.div(slot, row_tiles) ^ me
        block = shards[0][:, held]
        for d in range(1, helpers):
            block = jnp.where(step == d, shards[d][:, held], block)
        out[:, :, j * side:(j + 1) * side] = block
    volumes, steps, vectors, _ = gram.shape
    total = jnp.sum(parts[...].astype(jnp.float32), axis=0) * scale
    for step in range(steps):
        for v in range(volumes):
            at = (step * volumes + v) * vectors
            gram[v, step] = total[:, at:at + vectors]


def tile_pair(tiles, j, k):
    return jnp.concatenate(
        [jnp.concatenate([tiles[v, j, k], tiles[v, j, k + 1]], axis=1) for v in range(tiles.shape[0])],
        axis=0,
    )


def near_block(ints, ext, j, k, slab_size, ghosts, row_tiles, odd, lead):
    col = ints[j, k]
    side = jnp.where(col >= slab_size + ghosts, 1, 0)
    near = jnp.logical_or(col < slab_size, side != odd)
    used = jnp.logical_and(near, k < ints[row_tiles, j])
    return jnp.where(used, ext[lead + (col,)], 0).astype(ext.dtype)


def make_table(ints, built, row_tiles, slots, slab_size, ghosts, odd):
    low = slab_size + odd * ghosts
    found = jnp.int32(0)
    for j in range(row_tiles):
        live = ints[row_tiles, j]
        for k in range(slots):
            ghost = ints[j, k] - low
            built[0, found] = (j * slots + k) * ghosts + ghost
            crosses = jnp.logical_and(jnp.logical_and(ghost >= 0, ghost < ghosts), k < live)
            found += jnp.where(crosses, 1, 0)
    built[1, 0] = found
    for q in range(slab_size):
        built[4, ints[row_tiles + 1, q]] = q
    pair_rows, cross_rows = ghost_rows(ints, row_tiles, odd)
    for g in range(ghosts):
        built[2, g] = built[4, pair_rows[0, g]]
        built[3, g] = built[4, cross_rows[0, g]]


def near_first(ints, slab, pair, tiles, part, stored, table, ext, built, done):
    volumes, row_tiles, slots, side, _ = tiles.shape
    slab_size, ghosts, vectors = slab.shape[0], pair.shape[0], slab.shape[1]
    me = lax.axis_index("help")
    odd = lax.rem(lax.axis_index("rows"), 2)
    make_table(ints, built, row_tiles, slots, slab_size, ghosts, odd)
    hand_over = pltpu.make_async_copy(built, table, done)
    hand_over.start()
    ext[pl.ds(0, slab_size)] = slab[...]
    ext[pl.ds(slab_size + (1 - odd) * ghosts, ghosts)] = pair[...]
    mine = rolled(ints[row_tiles + 1:row_tiles + 2, :], me * row_tiles)
    for j in range(row_tiles):
        total = jnp.zeros((vectors, volumes * side), jnp.float32)
        for k in range(0, slots, 2):
            left = jnp.concatenate(
                [near_block(ints, ext, j, q, slab_size, ghosts, row_tiles, odd, ()) for q in (k, k + 1)], axis=1
            )
            total += lax.dot_general(left, tile_pair(tiles, j, k), NT, preferred_element_type=jnp.float32)
        for v in range(volumes):
            part[v, j] = total[:, v * side:(v + 1) * side]
        stored[j] = slab[mine[0, j]]
    hand_over.wait()


def near_second(ints, slab, pair, tiles, part, ext):
    volumes, row_tiles, slots, side, _ = tiles.shape
    slab_size, ghosts, vectors = slab.shape[1], pair.shape[1], slab.shape[2]
    odd = lax.rem(lax.axis_index("rows"), 2)
    for q in range(slab_size):
        ext[:, ints[row_tiles + 1, q]] = slab[:, q]
    ext[:, pl.ds(slab_size + (1 - odd) * ghosts, ghosts)] = pair[...]
    for j in range(row_tiles):
        total = jnp.zeros((volumes * vectors, volumes * side), jnp.float32)
        for k in range(0, slots, 2):
            left = jnp.concatenate(
                [
                    jnp.concatenate(
                        [
                            near_block(ints, ext, j, q, slab_size, ghosts, row_tiles, odd, (v,))
                            for q in (k, k + 1)
                        ],
                        axis=1,
                    )
                    for v in range(volumes)
                ],
                axis=0,
            )
            total += lax.dot_general(left, tile_pair(tiles, j, k), NT, preferred_element_type=jnp.float32)
        for v in range(volumes):
            part[v, j] = total[v * vectors:(v + 1) * vectors, v * side:(v + 1) * side]


def add_cross(table, cross, tiles, acc, lead):
    volumes, row_tiles, slots, side, _ = tiles.shape
    ghosts = cross.shape[len(lead)]
    items = table[0:1, :]
    found = table[1, 0]

    def chunk_items(i):
        row = rolled(items, lax.rem(i * CHUNK, LANES))
        return tuple(row[0, u] for u in range(CHUNK))

    def chunk(i, held):
        products = []
        for u in range(CHUNK):
            used = i * CHUNK + u < found
            item = jnp.where(used, held[u], 0)
            tile = lax.div(item, ghosts)
            g = lax.rem(item, ghosts)
            j = lax.div(tile, slots)
            k = lax.rem(tile, slots)
            if lead:
                blocks = jnp.concatenate([cross[v, g] for v in range(volumes)], axis=0)
            else:
                blocks = cross[g]
            blocks = jnp.where(used, blocks, 0).astype(cross.dtype)
            weights = jnp.concatenate([tiles[v, j, k] for v in range(volumes)], axis=0)
            products.append((j, lax.dot_general(blocks, weights, NT, preferred_element_type=jnp.float32)))
        following = chunk_items(i + 1)
        for j, product in products:
            for v in range(volumes):
                rows = product.shape[0] // volumes if lead else product.shape[0]
                low = v * rows if lead else 0
                acc[v, j] += product[low:low + rows, v * side:(v + 1) * side]
        return following

    lax.fori_loop(0, lax.div(found + CHUNK - 1, CHUNK), chunk, chunk_items(jnp.int32(0)))


def apply_first(coefs, table, stored, cross, tiles, part, first, gram, acc):
    volumes, row_tiles = first.shape[:2]
    acc[...] = part[...]
    add_cross(table, cross, tiles, acc, ())
    for v in range(volumes):
        centre = coefs[v:v + 1, :]
        scale = 1.0 / coefs[volumes + v:volumes + v + 1, :]
        for j in range(row_tiles):
            first[v, j] = ((acc[v, j] - centre * stored[j].astype(jnp.float32)) * scale).astype(first.dtype)
        field = jnp.concatenate([first[v, j] for j in range(row_tiles)], axis=1)
        gram[v] = lax.dot_general(field, field, NT, preferred_element_type=jnp.float32)


def apply_second(coefs, table, stored, cross, tiles, part, first, gram_one, second, gram, acc):
    volumes, row_tiles = first.shape[:2]
    acc[...] = part[...]
    add_cross(table, cross, tiles, acc, (0,))
    parts = [gram_one[v] for v in range(volumes)]
    for v in range(volumes):
        centre = coefs[v:v + 1, :]
        scale = 2.0 / coefs[volumes + v:volumes + v + 1, :]
        for j in range(row_tiles):
            inner = acc[v, j] - centre * first[v, j].astype(jnp.float32)
            second[v, j] = (inner * scale - stored[j].astype(jnp.float32)).astype(second.dtype)
        field = jnp.concatenate([second[v, j] for j in range(row_tiles)], axis=1)
        parts.append(lax.dot_general(field, field, NT, preferred_element_type=jnp.float32))
    gram[...] = jnp.concatenate(parts, axis=1)


def summed_parts(value, groups):
    parts = jnp.broadcast_to(value.astype(jnp.bfloat16)[None], (len(groups[0]),) + value.shape)
    return lax.all_to_all(parts, ("rows", "help"), 0, 0, axis_index_groups=groups)


def per_device(panel, tiles, tile_cols, tile_count, row_assign, send_lists, centers, half_widths):
    helpers = lax.axis_size("help")
    rows = lax.axis_size("rows")
    volumes, row_tiles, slots, side, _ = tiles.shape
    vectors = panel.shape[0]
    ghosts = send_lists.shape[2]
    slab_size = row_tiles * helpers
    bf16 = panel.dtype
    depth = rows // (SIDE_CHIPS * CORES)

    def at(z, y, core, x):
        return ((z * SIDE_CHIPS + y) * CORES + core) * helpers + x

    def shape(*dims):
        return jax.ShapeDtypeStruct(dims, bf16)

    def gathered(shard):
        others = [
            lax.ppermute(shard, "help", [(i, i ^ d) for i in range(helpers)]) for d in range(1, helpers)
        ]
        return [shard] + others

    def exchanged(to_pair, to_cross):
        cross_pairs = [(s, (s + 1) % rows if s % 2 else (s - 1) % rows) for s in range(rows)]
        cross = lax.ppermute(to_cross, "rows", cross_pairs)
        pair = lax.ppermute(to_pair, "rows", [(s, s ^ 1) for s in range(rows)])
        return pair, cross

    params = pltpu.CompilerParams(vmem_limit_bytes=24 * 1024 * 1024)

    ints = jnp.concatenate(
        [
            jnp.pad(tile_cols, ((0, 0), (0, LANES - slots))),
            jnp.pad(tile_count[None], ((0, 0), (0, LANES - row_tiles))),
            jnp.pad(row_assign[None], ((0, 0), (0, LANES - slab_size))),
            jnp.pad(send_lists[0], ((0, 0), (0, LANES - ghosts))),
        ],
        axis=0,
    )
    coefs = jnp.broadcast_to(jnp.concatenate([centers, half_widths])[:, None], (2 * volumes, LANES))
    own_panel = pl.pallas_call(
        own_blocks,
        out_shape=shape(row_tiles, vectors, side),
        in_specs=[VMEM] * 2,
        out_specs=VMEM,
        compiler_params=params,
        name="own_blocks",
    )(panel, tiles)
    base, to_pair, to_cross = pl.pallas_call(
        functools.partial(spread_panel, helpers),
        out_shape=[shape(slab_size, vectors, side)] + [shape(ghosts, vectors, side)] * 2,
        in_specs=[VMEM] * (1 + helpers),
        out_specs=[VMEM] * 3,
        compiler_params=params,
        name="spread_panel",
    )(ints, own_panel, *gathered(panel)[1:])
    pair, cross = exchanged(to_pair, to_cross)
    part_shape = jax.ShapeDtypeStruct((volumes, row_tiles, vectors, side), jnp.float32)
    product_cost = pl.CostEstimate(
        flops=4 * volumes * row_tiles * slots * side * side * vectors,
        bytes_accessed=2 * tiles.size,
        transcendentals=0,
    )
    table_shape = (5, LANES)
    part, stored, table = pl.pallas_call(
        near_first,
        out_shape=[
            part_shape,
            shape(row_tiles, vectors, side),
            jax.ShapeDtypeStruct(table_shape, jnp.int32),
        ],
        in_specs=[VMEM] * 4,
        out_specs=[VMEM] * 3,
        scratch_shapes=[
            pltpu.VMEM((slab_size + 2 * ghosts, vectors, side), bf16),
            pltpu.SMEM(table_shape, jnp.int32),
            pltpu.SemaphoreType.DMA,
        ],
        compiler_params=params,
        cost_estimate=product_cost,
        name="near_first",
    )(ints, base, pair, tiles)
    first, gram_one = pl.pallas_call(
        apply_first,
        out_shape=[
            shape(volumes, row_tiles, vectors, side),
            jax.ShapeDtypeStruct((volumes, vectors, vectors), jnp.float32),
        ],
        in_specs=[VMEM] * 6,
        out_specs=[VMEM] * 2,
        scratch_shapes=[pltpu.VMEM(part_shape.shape, jnp.float32)],
        compiler_params=params,
        name="apply_first",
    )(coefs, table, stored, cross, tiles, part)
    slab, to_pair, to_cross = pl.pallas_call(
        functools.partial(spread_field, helpers),
        out_shape=[shape(volumes, slab_size, vectors, side)] + [shape(volumes, ghosts, vectors, side)] * 2,
        in_specs=[VMEM] * (1 + helpers),
        out_specs=[VMEM] * 3,
        compiler_params=params,
        name="spread_field",
    )(table, *gathered(first))
    pair, cross = exchanged(to_pair, to_cross)
    part = pl.pallas_call(
        near_second,
        out_shape=part_shape,
        in_specs=[VMEM] * 4,
        out_specs=VMEM,
        scratch_shapes=[pltpu.VMEM((volumes, slab_size + 2 * ghosts, vectors, side), bf16)],
        compiler_params=params,
        cost_estimate=product_cost,
        name="near_second",
    )(ints, slab, pair, tiles)
    second, gram = pl.pallas_call(
        apply_second,
        out_shape=[
            shape(volumes, row_tiles, vectors, side),
            jax.ShapeDtypeStruct((vectors, 2 * volumes * vectors), jnp.float32),
        ],
        in_specs=[VMEM] * 8,
        out_specs=[VMEM] * 2,
        scratch_shapes=[pltpu.VMEM(part_shape.shape, jnp.float32)],
        compiler_params=params,
        name="apply_second",
    )(coefs, table, stored, cross, tiles, part, first, gram_one)

    near = [
        [at(z, y, c, x) for y in range(SIDE_CHIPS) for x in range(helpers)]
        for z in range(depth)
        for c in range(CORES)
    ]
    far = [
        [at(z, y, c, x) for z in range(depth) for c in range(CORES)]
        for y in range(SIDE_CHIPS)
        for x in range(helpers)
    ]
    gram = jnp.sum(summed_parts(gram, near).astype(jnp.float32), axis=0)
    gram, late = lax.optimization_barrier((gram, second))
    shards = gathered(late)
    parts = summed_parts(gram, far)
    filtered, gram = pl.pallas_call(
        functools.partial(finish, helpers, 1.0 / (row_tiles * side * helpers * rows)),
        out_shape=[
            shape(volumes, vectors, row_tiles * side),
            jax.ShapeDtypeStruct((volumes, 2, vectors, vectors), jnp.float32),
        ],
        in_specs=[VMEM] * (2 + helpers),
        out_specs=[VMEM] * 2,
        compiler_params=params,
        name="finish",
    )(table, parts, *shards)
    return filtered, gram


def solution(mesh):
    placed = (
        P(None, ("rows", "help")),
        P(None, ("rows", "help"), None, None, None),
        P(("rows", "help"), None),
        P(("rows", "help")),
        P("rows"),
        P("rows", None, None),
        P(),
        P(),
    )
    return jax.shard_map(
        per_device,
        mesh=mesh,
        in_specs=placed,
        out_specs=(P(None, None, ("rows", "help")), P()),
        check_vma=False,
    )
```

```python
import functools

import jax
import jax.numpy as jnp
from jax import lax
from jax.experimental import pallas as pl
from jax.experimental.pallas import tpu as pltpu
from jax.sharding import PartitionSpec as P

CORES = 2
LANES = 128
CHUNK = 8
SIDE_CHIPS = 4
NT = (((1,), (1,)), ((), ()))
VMEM = pl.BlockSpec(memory_space=pltpu.VMEM)


def own_blocks(panel, tiles, blocks):
    side = blocks.shape[2]
    for j in range(blocks.shape[0]):
        blocks[j] = panel[:, j * side:(j + 1) * side]


def rolled(row, first):
    return pltpu.roll(row, lax.rem(row.shape[1] - first, row.shape[1]), 1)


def ghost_rows(ints, row_tiles, odd):
    to_prev = ints[row_tiles + 2:row_tiles + 3, :]
    to_next = ints[row_tiles + 3:row_tiles + 4, :]
    return jnp.where(odd == 1, to_prev, to_next), jnp.where(odd == 1, to_next, to_prev)


def spread_panel(helpers, ints, *refs):
    shards, (slab, to_pair, to_cross) = refs[:helpers], refs[helpers:]
    me = lax.axis_index("help")
    odd = lax.rem(lax.axis_index("rows"), 2)
    side = slab.shape[2]
    row_tiles = slab.shape[0] // helpers
    for d in range(helpers):
        base = (me ^ d) * row_tiles
        for j in range(row_tiles):
            slab[base + j] = shards[d][:, j * side:(j + 1) * side] if d else shards[0][j]
    pair_rows, cross_rows = ghost_rows(ints, row_tiles, odd)
    for g in range(to_pair.shape[0]):
        to_cross[g] = slab[cross_rows[0, g]]
        to_pair[g] = slab[pair_rows[0, g]]


def spread_field(helpers, table, *refs):
    shards, (slab, to_pair, to_cross) = refs[:helpers], refs[helpers:]
    me = lax.axis_index("help")
    row_tiles = slab.shape[1] // helpers
    for d in range(helpers):
        slab[:, pl.ds((me ^ d) * row_tiles, row_tiles)] = shards[d][...]
    for g in range(to_pair.shape[1]):
        to_cross[:, g] = slab[:, table[3, g]]
        to_pair[:, g] = slab[:, table[2, g]]


def finish(helpers, scale, table, parts, *refs):
    shards, (out, gram) = refs[:helpers], refs[helpers:]
    me = lax.axis_index("help")
    row_tiles, side = shards[0].shape[1], shards[0].shape[3]
    slots = rolled(table[4:5, :], me * row_tiles)
    for j in range(row_tiles):
        slot = slots[0, j]
        held = lax.rem(slot, row_tiles)
        step = lax.div(slot, row_tiles) ^ me
        block = shards[0][:, held]
        for d in range(1, helpers):
            block = jnp.where(step == d, shards[d][:, held], block)
        out[:, :, j * side:(j + 1) * side] = block
    volumes, steps, vectors, _ = gram.shape
    total = jnp.sum(parts[...].astype(jnp.float32), axis=0) * scale
    for step in range(steps):
        for v in range(volumes):
            at = (step * volumes + v) * vectors
            gram[v, step] = total[:, at:at + vectors]


def tile_pair(tiles, j, k):
    return jnp.concatenate(
        [jnp.concatenate([tiles[v, j, k], tiles[v, j, k + 1]], axis=1) for v in range(tiles.shape[0])],
        axis=0,
    )


def near_block(ints, ext, j, k, slab_size, ghosts, row_tiles, odd, lead):
    col = ints[j, k]
    side = jnp.where(col >= slab_size + ghosts, 1, 0)
    near = jnp.logical_or(col < slab_size, side != odd)
    used = jnp.logical_and(near, k < ints[row_tiles, j])
    return jnp.where(used, ext[lead + (col,)], 0).astype(ext.dtype)


def list_row(ints, built, found, j, row_tiles, slots, slab_size, ghosts, odd):
    low = slab_size + odd * ghosts
    live = ints[row_tiles, j]
    for k in range(slots):
        ghost = ints[j, k] - low
        built[0, found] = (j * slots + k) * ghosts + ghost
        crosses = jnp.logical_and(jnp.logical_and(ghost >= 0, ghost < ghosts), k < live)
        found += jnp.where(crosses, 1, 0)
    return found


def near_first(ints, slab, pair, tiles, part, stored, table, ext, built, done):
    volumes, row_tiles, slots, side, _ = tiles.shape
    slab_size, ghosts, vectors = slab.shape[0], pair.shape[0], slab.shape[1]
    me = lax.axis_index("help")
    odd = lax.rem(lax.axis_index("rows"), 2)
    ext[pl.ds(0, slab_size)] = slab[...]
    ext[pl.ds(slab_size + (1 - odd) * ghosts, ghosts)] = pair[...]
    mine = rolled(ints[row_tiles + 1:row_tiles + 2, :], me * row_tiles)
    pair_rows, cross_rows = ghost_rows(ints, row_tiles, odd)
    found = jnp.int32(0)
    half = row_tiles // 2
    hand_over = pltpu.make_async_copy(built, table, done)
    for j in range(row_tiles):
        if j < half:
            for q in range(j * slab_size // half, (j + 1) * slab_size // half):
                built[4, ints[row_tiles + 1, q]] = q
            for row in (2 * j, 2 * j + 1):
                found = list_row(ints, built, found, row, row_tiles, slots, slab_size, ghosts, odd)
        if j == half:
            built[1, 0] = found
            for g in range(ghosts):
                built[2, g] = built[4, pair_rows[0, g]]
                built[3, g] = built[4, cross_rows[0, g]]
            hand_over.start()
        total = jnp.zeros((vectors, volumes * side), jnp.float32)
        for k in range(0, slots, 2):
            left = jnp.concatenate(
                [near_block(ints, ext, j, q, slab_size, ghosts, row_tiles, odd, ()) for q in (k, k + 1)], axis=1
            )
            total += lax.dot_general(left, tile_pair(tiles, j, k), NT, preferred_element_type=jnp.float32)
        for v in range(volumes):
            part[v, j] = total[:, v * side:(v + 1) * side]
        stored[j] = slab[mine[0, j]]
    hand_over.wait()


def near_second(ints, slab, pair, tiles, part, ext):
    volumes, row_tiles, slots, side, _ = tiles.shape
    slab_size, ghosts, vectors = slab.shape[1], pair.shape[1], slab.shape[2]
    odd = lax.rem(lax.axis_index("rows"), 2)
    for q in range(slab_size):
        ext[:, ints[row_tiles + 1, q]] = slab[:, q]
    ext[:, pl.ds(slab_size + (1 - odd) * ghosts, ghosts)] = pair[...]
    for j in range(row_tiles):
        total = jnp.zeros((volumes * vectors, volumes * side), jnp.float32)
        for k in range(0, slots, 2):
            left = jnp.concatenate(
                [
                    jnp.concatenate(
                        [
                            near_block(ints, ext, j, q, slab_size, ghosts, row_tiles, odd, (v,))
                            for q in (k, k + 1)
                        ],
                        axis=1,
                    )
                    for v in range(volumes)
                ],
                axis=0,
            )
            total += lax.dot_general(left, tile_pair(tiles, j, k), NT, preferred_element_type=jnp.float32)
        for v in range(volumes):
            part[v, j] = total[v * vectors:(v + 1) * vectors, v * side:(v + 1) * side]


def add_cross(table, cross, tiles, acc, lead):
    volumes, row_tiles, slots, side, _ = tiles.shape
    ghosts = cross.shape[len(lead)]
    items = table[0:1, :]
    found = table[1, 0]

    def chunk_items(i):
        row = rolled(items, lax.rem(i * CHUNK, LANES))
        return tuple(row[0, u] for u in range(CHUNK))

    def chunk(i, held):
        products = []
        for u in range(CHUNK):
            used = i * CHUNK + u < found
            item = jnp.where(used, held[u], 0)
            tile = lax.div(item, ghosts)
            g = lax.rem(item, ghosts)
            j = lax.div(tile, slots)
            k = lax.rem(tile, slots)
            if lead:
                blocks = jnp.concatenate([cross[v, g] for v in range(volumes)], axis=0)
            else:
                blocks = cross[g]
            blocks = jnp.where(used, blocks, 0).astype(cross.dtype)
            weights = jnp.concatenate([tiles[v, j, k] for v in range(volumes)], axis=0)
            products.append((j, lax.dot_general(blocks, weights, NT, preferred_element_type=jnp.float32)))
        following = chunk_items(i + 1)
        for j, product in products:
            for v in range(volumes):
                rows = product.shape[0] // volumes if lead else product.shape[0]
                low = v * rows if lead else 0
                acc[v, j] += product[low:low + rows, v * side:(v + 1) * side]
        return following

    lax.fori_loop(0, lax.div(found + CHUNK - 1, CHUNK), chunk, chunk_items(jnp.int32(0)))


def apply_first(coefs, table, stored, cross, tiles, part, first, gram, acc):
    volumes, row_tiles = first.shape[:2]
    acc[...] = part[...]
    add_cross(table, cross, tiles, acc, ())
    for v in range(volumes):
        centre = coefs[v:v + 1, :]
        scale = 1.0 / coefs[volumes + v:volumes + v + 1, :]
        for j in range(row_tiles):
            first[v, j] = ((acc[v, j] - centre * stored[j].astype(jnp.float32)) * scale).astype(first.dtype)
        field = jnp.concatenate([first[v, j] for j in range(row_tiles)], axis=1)
        gram[v] = lax.dot_general(field, field, NT, preferred_element_type=jnp.float32)


def apply_second(coefs, table, stored, cross, tiles, part, first, gram_one, second, gram, acc):
    volumes, row_tiles = first.shape[:2]
    acc[...] = part[...]
    add_cross(table, cross, tiles, acc, (0,))
    parts = [gram_one[v] for v in range(volumes)]
    for v in range(volumes):
        centre = coefs[v:v + 1, :]
        scale = 2.0 / coefs[volumes + v:volumes + v + 1, :]
        for j in range(row_tiles):
            inner = acc[v, j] - centre * first[v, j].astype(jnp.float32)
            second[v, j] = (inner * scale - stored[j].astype(jnp.float32)).astype(second.dtype)
        field = jnp.concatenate([second[v, j] for j in range(row_tiles)], axis=1)
        parts.append(lax.dot_general(field, field, NT, preferred_element_type=jnp.float32))
    gram[...] = jnp.concatenate(parts, axis=1)


def summed_parts(value, groups):
    parts = jnp.broadcast_to(value.astype(jnp.bfloat16)[None], (len(groups[0]),) + value.shape)
    return lax.all_to_all(parts, ("rows", "help"), 0, 0, axis_index_groups=groups)


def per_device(panel, tiles, tile_cols, tile_count, row_assign, send_lists, centers, half_widths):
    helpers = lax.axis_size("help")
    rows = lax.axis_size("rows")
    volumes, row_tiles, slots, side, _ = tiles.shape
    vectors = panel.shape[0]
    ghosts = send_lists.shape[2]
    slab_size = row_tiles * helpers
    bf16 = panel.dtype
    depth = rows // (SIDE_CHIPS * CORES)

    def at(z, y, core, x):
        return ((z * SIDE_CHIPS + y) * CORES + core) * helpers + x

    def shape(*dims):
        return jax.ShapeDtypeStruct(dims, bf16)

    def gathered(shard):
        others = [
            lax.ppermute(shard, "help", [(i, i ^ d) for i in range(helpers)]) for d in range(1, helpers)
        ]
        return [shard] + others

    def exchanged(to_pair, to_cross):
        cross_pairs = [(s, (s + 1) % rows if s % 2 else (s - 1) % rows) for s in range(rows)]
        cross = lax.ppermute(to_cross, "rows", cross_pairs)
        pair = lax.ppermute(to_pair, "rows", [(s, s ^ 1) for s in range(rows)])
        return pair, cross

    params = pltpu.CompilerParams(vmem_limit_bytes=24 * 1024 * 1024)

    ints = jnp.concatenate(
        [
            jnp.pad(tile_cols, ((0, 0), (0, LANES - slots))),
            jnp.pad(tile_count[None], ((0, 0), (0, LANES - row_tiles))),
            jnp.pad(row_assign[None], ((0, 0), (0, LANES - slab_size))),
            jnp.pad(send_lists[0], ((0, 0), (0, LANES - ghosts))),
        ],
        axis=0,
    )
    coefs = jnp.broadcast_to(jnp.concatenate([centers, half_widths])[:, None], (2 * volumes, LANES))
    own_panel = pl.pallas_call(
        own_blocks,
        out_shape=shape(row_tiles, vectors, side),
        in_specs=[VMEM] * 2,
        out_specs=VMEM,
        compiler_params=params,
        name="own_blocks",
    )(panel, tiles)
    base, to_pair, to_cross = pl.pallas_call(
        functools.partial(spread_panel, helpers),
        out_shape=[shape(slab_size, vectors, side)] + [shape(ghosts, vectors, side)] * 2,
        in_specs=[VMEM] * (1 + helpers),
        out_specs=[VMEM] * 3,
        compiler_params=params,
        name="spread_panel",
    )(ints, own_panel, *gathered(panel)[1:])
    pair, cross = exchanged(to_pair, to_cross)
    part_shape = jax.ShapeDtypeStruct((volumes, row_tiles, vectors, side), jnp.float32)
    product_cost = pl.CostEstimate(
        flops=4 * volumes * row_tiles * slots * side * side * vectors,
        bytes_accessed=2 * tiles.size,
        transcendentals=0,
    )
    table_shape = (5, LANES)
    part, stored, table = pl.pallas_call(
        near_first,
        out_shape=[
            part_shape,
            shape(row_tiles, vectors, side),
            jax.ShapeDtypeStruct(table_shape, jnp.int32),
        ],
        in_specs=[VMEM] * 4,
        out_specs=[VMEM] * 3,
        scratch_shapes=[
            pltpu.VMEM((slab_size + 2 * ghosts, vectors, side), bf16),
            pltpu.SMEM(table_shape, jnp.int32),
            pltpu.SemaphoreType.DMA,
        ],
        compiler_params=params,
        cost_estimate=product_cost,
        name="near_first",
    )(ints, base, pair, tiles)
    first, gram_one = pl.pallas_call(
        apply_first,
        out_shape=[
            shape(volumes, row_tiles, vectors, side),
            jax.ShapeDtypeStruct((volumes, vectors, vectors), jnp.float32),
        ],
        in_specs=[VMEM] * 6,
        out_specs=[VMEM] * 2,
        scratch_shapes=[pltpu.VMEM(part_shape.shape, jnp.float32)],
        compiler_params=params,
        name="apply_first",
    )(coefs, table, stored, cross, tiles, part)
    slab, to_pair, to_cross = pl.pallas_call(
        functools.partial(spread_field, helpers),
        out_shape=[shape(volumes, slab_size, vectors, side)] + [shape(volumes, ghosts, vectors, side)] * 2,
        in_specs=[VMEM] * (1 + helpers),
        out_specs=[VMEM] * 3,
        compiler_params=params,
        name="spread_field",
    )(table, *gathered(first))
    pair, cross = exchanged(to_pair, to_cross)
    part = pl.pallas_call(
        near_second,
        out_shape=part_shape,
        in_specs=[VMEM] * 4,
        out_specs=VMEM,
        scratch_shapes=[pltpu.VMEM((volumes, slab_size + 2 * ghosts, vectors, side), bf16)],
        compiler_params=params,
        cost_estimate=product_cost,
        name="near_second",
    )(ints, slab, pair, tiles)
    second, gram = pl.pallas_call(
        apply_second,
        out_shape=[
            shape(volumes, row_tiles, vectors, side),
            jax.ShapeDtypeStruct((vectors, 2 * volumes * vectors), jnp.float32),
        ],
        in_specs=[VMEM] * 8,
        out_specs=[VMEM] * 2,
        scratch_shapes=[pltpu.VMEM(part_shape.shape, jnp.float32)],
        compiler_params=params,
        name="apply_second",
    )(coefs, table, stored, cross, tiles, part, first, gram_one)

    near = [
        [at(z, y, c, x) for y in range(SIDE_CHIPS) for x in range(helpers)]
        for z in range(depth)
        for c in range(CORES)
    ]
    far = [
        [at(z, y, c, x) for z in range(depth) for c in range(CORES)]
        for y in range(SIDE_CHIPS)
        for x in range(helpers)
    ]
    gram = jnp.sum(summed_parts(gram, near).astype(jnp.float32), axis=0)
    gram, late = lax.optimization_barrier((gram, second))
    shards = gathered(late)
    parts = summed_parts(gram, far)
    filtered, gram = pl.pallas_call(
        functools.partial(finish, helpers, 1.0 / (row_tiles * side * helpers * rows)),
        out_shape=[
            shape(volumes, vectors, row_tiles * side),
            jax.ShapeDtypeStruct((volumes, 2, vectors, vectors), jnp.float32),
        ],
        in_specs=[VMEM] * (2 + helpers),
        out_specs=[VMEM] * 2,
        compiler_params=params,
        name="finish",
    )(table, parts, *shards)
    return filtered, gram


def solution(mesh):
    placed = (
        P(None, ("rows", "help")),
        P(None, ("rows", "help"), None, None, None),
        P(("rows", "help"), None),
        P(("rows", "help")),
        P("rows"),
        P("rows", None, None),
        P(),
        P(),
    )
    return jax.shard_map(
        per_device,
        mesh=mesh,
        in_specs=placed,
        out_specs=(P(None, None, ("rows", "help")), P()),
        check_vma=False,
    )
```

```python
import functools

import jax
import jax.numpy as jnp
from jax import lax
from jax.experimental import pallas as pl
from jax.experimental.pallas import tpu as pltpu
from jax.sharding import PartitionSpec as P

CORES = 2
LANES = 128
CHUNK = 8
SIDE_CHIPS = 4
NT = (((1,), (1,)), ((), ()))
VMEM = pl.BlockSpec(memory_space=pltpu.VMEM)


def own_blocks(panel, tiles, blocks):
    side = blocks.shape[2]
    for j in range(blocks.shape[0]):
        blocks[j] = panel[:, j * side:(j + 1) * side]


def distances(helpers):
    return sorted(range(helpers), key=lambda d: min(d, helpers - d))


def rolled(row, first):
    return pltpu.roll(row, lax.rem(row.shape[1] - first, row.shape[1]), 1)


def ghost_rows(ints, row_tiles, odd):
    to_prev = ints[row_tiles + 2:row_tiles + 3, :]
    to_next = ints[row_tiles + 3:row_tiles + 4, :]
    return jnp.where(odd == 1, to_prev, to_next), jnp.where(odd == 1, to_next, to_prev)


def spread_panel(helpers, ints, *refs):
    shards, (slab, to_pair, to_cross) = refs[:helpers], refs[helpers:]
    me = lax.axis_index("help")
    odd = lax.rem(lax.axis_index("rows"), 2)
    side = slab.shape[2]
    row_tiles = slab.shape[0] // helpers
    for at, d in enumerate(distances(helpers)):
        base = (me ^ d) * row_tiles
        for j in range(row_tiles):
            slab[base + j] = shards[at][:, j * side:(j + 1) * side] if d else shards[0][j]
    pair_rows, cross_rows = ghost_rows(ints, row_tiles, odd)
    for g in range(to_pair.shape[0]):
        to_cross[g] = slab[cross_rows[0, g]]
        to_pair[g] = slab[pair_rows[0, g]]


def spread_field(helpers, table, *refs):
    shards, (slab, to_pair, to_cross) = refs[:helpers], refs[helpers:]
    me = lax.axis_index("help")
    row_tiles = slab.shape[1] // helpers
    for at, d in enumerate(distances(helpers)):
        slab[:, pl.ds((me ^ d) * row_tiles, row_tiles)] = shards[at][...]
    for g in range(to_pair.shape[1]):
        to_cross[:, g] = slab[:, table[3, g]]
        to_pair[:, g] = slab[:, table[2, g]]


def finish(helpers, scale, table, parts, *refs):
    shards, (out, gram) = refs[:helpers], refs[helpers:]
    me = lax.axis_index("help")
    row_tiles, side = shards[0].shape[1], shards[0].shape[3]
    slots = rolled(table[4:5, :], me * row_tiles)
    for j in range(row_tiles):
        slot = slots[0, j]
        held = lax.rem(slot, row_tiles)
        step = lax.div(slot, row_tiles) ^ me
        block = shards[0][:, held]
        for at, d in enumerate(distances(helpers)):
            block = jnp.where(step == d, shards[at][:, held], block)
        out[:, :, j * side:(j + 1) * side] = block
    volumes, steps, vectors, _ = gram.shape
    total = jnp.sum(parts[...].astype(jnp.float32), axis=0) * scale
    for step in range(steps):
        for v in range(volumes):
            at = (step * volumes + v) * vectors
            gram[v, step] = total[:, at:at + vectors]


def tile_pair(tiles, j, k):
    return jnp.concatenate(
        [jnp.concatenate([tiles[v, j, k], tiles[v, j, k + 1]], axis=1) for v in range(tiles.shape[0])],
        axis=0,
    )


def near_block(ints, ext, j, k, slab_size, ghosts, row_tiles, odd, lead):
    col = ints[j, k]
    side = jnp.where(col >= slab_size + ghosts, 1, 0)
    near = jnp.logical_or(col < slab_size, side != odd)
    used = jnp.logical_and(near, k < ints[row_tiles, j])
    return jnp.where(used, ext[lead + (col,)], 0).astype(ext.dtype)


def list_row(ints, built, found, j, row_tiles, slots, slab_size, ghosts, odd):
    low = slab_size + odd * ghosts
    live = ints[row_tiles, j]
    for k in range(slots):
        ghost = ints[j, k] - low
        built[0, found] = (j * slots + k) * ghosts + ghost
        crosses = jnp.logical_and(jnp.logical_and(ghost >= 0, ghost < ghosts), k < live)
        found += jnp.where(crosses, 1, 0)
    return found


def near_first(ints, slab, pair, tiles, part, stored, table, ext, built, done):
    volumes, row_tiles, slots, side, _ = tiles.shape
    slab_size, ghosts, vectors = slab.shape[0], pair.shape[0], slab.shape[1]
    me = lax.axis_index("help")
    odd = lax.rem(lax.axis_index("rows"), 2)
    ext[pl.ds(0, slab_size)] = slab[...]
    ext[pl.ds(slab_size + (1 - odd) * ghosts, ghosts)] = pair[...]
    mine = rolled(ints[row_tiles + 1:row_tiles + 2, :], me * row_tiles)
    pair_rows, cross_rows = ghost_rows(ints, row_tiles, odd)
    found = jnp.int32(0)
    half = row_tiles // 2
    hand_over = pltpu.make_async_copy(built, table, done)
    for j in range(row_tiles):
        if j < half:
            for q in range(j * slab_size // half, (j + 1) * slab_size // half):
                built[4, ints[row_tiles + 1, q]] = q
            for row in (2 * j, 2 * j + 1):
                found = list_row(ints, built, found, row, row_tiles, slots, slab_size, ghosts, odd)
        if j == half:
            built[1, 0] = found
            for g in range(ghosts):
                built[2, g] = built[4, pair_rows[0, g]]
                built[3, g] = built[4, cross_rows[0, g]]
            hand_over.start()
        total = jnp.zeros((vectors, volumes * side), jnp.float32)
        for k in range(0, slots, 2):
            left = jnp.concatenate(
                [near_block(ints, ext, j, q, slab_size, ghosts, row_tiles, odd, ()) for q in (k, k + 1)], axis=1
            )
            total += lax.dot_general(left, tile_pair(tiles, j, k), NT, preferred_element_type=jnp.float32)
        for v in range(volumes):
            part[v, j] = total[:, v * side:(v + 1) * side]
        stored[j] = slab[mine[0, j]]
    hand_over.wait()


def near_second(ints, slab, pair, tiles, part, ext):
    volumes, row_tiles, slots, side, _ = tiles.shape
    slab_size, ghosts, vectors = slab.shape[1], pair.shape[1], slab.shape[2]
    odd = lax.rem(lax.axis_index("rows"), 2)
    for q in range(slab_size):
        ext[:, ints[row_tiles + 1, q]] = slab[:, q]
    ext[:, pl.ds(slab_size + (1 - odd) * ghosts, ghosts)] = pair[...]
    for j in range(row_tiles):
        total = jnp.zeros((volumes * vectors, volumes * side), jnp.float32)
        for k in range(0, slots, 2):
            left = jnp.concatenate(
                [
                    jnp.concatenate(
                        [
                            near_block(ints, ext, j, q, slab_size, ghosts, row_tiles, odd, (v,))
                            for q in (k, k + 1)
                        ],
                        axis=1,
                    )
                    for v in range(volumes)
                ],
                axis=0,
            )
            total += lax.dot_general(left, tile_pair(tiles, j, k), NT, preferred_element_type=jnp.float32)
        for v in range(volumes):
            part[v, j] = total[v * vectors:(v + 1) * vectors, v * side:(v + 1) * side]


def add_cross(table, cross, tiles, acc, lead):
    volumes, row_tiles, slots, side, _ = tiles.shape
    ghosts = cross.shape[len(lead)]
    items = table[0:1, :]
    found = table[1, 0]

    def chunk_items(i):
        row = rolled(items, lax.rem(i * CHUNK, LANES))
        return tuple(row[0, u] for u in range(CHUNK))

    def chunk(i, held):
        products = []
        for u in range(CHUNK):
            used = i * CHUNK + u < found
            item = jnp.where(used, held[u], 0)
            tile = lax.div(item, ghosts)
            g = lax.rem(item, ghosts)
            j = lax.div(tile, slots)
            k = lax.rem(tile, slots)
            if lead:
                blocks = jnp.concatenate([cross[v, g] for v in range(volumes)], axis=0)
            else:
                blocks = cross[g]
            blocks = jnp.where(used, blocks, 0).astype(cross.dtype)
            weights = jnp.concatenate([tiles[v, j, k] for v in range(volumes)], axis=0)
            products.append((j, lax.dot_general(blocks, weights, NT, preferred_element_type=jnp.float32)))
        following = chunk_items(i + 1)
        for j, product in products:
            for v in range(volumes):
                rows = product.shape[0] // volumes if lead else product.shape[0]
                low = v * rows if lead else 0
                acc[v, j] += product[low:low + rows, v * side:(v + 1) * side]
        return following

    lax.fori_loop(0, lax.div(found + CHUNK - 1, CHUNK), chunk, chunk_items(jnp.int32(0)))


def apply_first(coefs, table, stored, cross, tiles, part, first, gram, acc):
    volumes, row_tiles = first.shape[:2]
    acc[...] = part[...]
    add_cross(table, cross, tiles, acc, ())
    for v in range(volumes):
        centre = coefs[v:v + 1, :]
        scale = 1.0 / coefs[volumes + v:volumes + v + 1, :]
        for j in range(row_tiles):
            first[v, j] = ((acc[v, j] - centre * stored[j].astype(jnp.float32)) * scale).astype(first.dtype)
        field = jnp.concatenate([first[v, j] for j in range(row_tiles)], axis=1)
        gram[v] = lax.dot_general(field, field, NT, preferred_element_type=jnp.float32)


def apply_second(coefs, table, stored, cross, tiles, part, first, gram_one, second, gram, acc):
    volumes, row_tiles = first.shape[:2]
    acc[...] = part[...]
    add_cross(table, cross, tiles, acc, (0,))
    parts = [gram_one[v] for v in range(volumes)]
    for v in range(volumes):
        centre = coefs[v:v + 1, :]
        scale = 2.0 / coefs[volumes + v:volumes + v + 1, :]
        for j in range(row_tiles):
            inner = acc[v, j] - centre * first[v, j].astype(jnp.float32)
            second[v, j] = (inner * scale - stored[j].astype(jnp.float32)).astype(second.dtype)
        field = jnp.concatenate([second[v, j] for j in range(row_tiles)], axis=1)
        parts.append(lax.dot_general(field, field, NT, preferred_element_type=jnp.float32))
    gram[...] = jnp.concatenate(parts, axis=1)


def summed_parts(value, groups):
    parts = jnp.broadcast_to(value.astype(jnp.bfloat16)[None], (len(groups[0]),) + value.shape)
    return lax.all_to_all(parts, ("rows", "help"), 0, 0, axis_index_groups=groups)


def per_device(panel, tiles, tile_cols, tile_count, row_assign, send_lists, centers, half_widths):
    helpers = lax.axis_size("help")
    rows = lax.axis_size("rows")
    volumes, row_tiles, slots, side, _ = tiles.shape
    vectors = panel.shape[0]
    ghosts = send_lists.shape[2]
    slab_size = row_tiles * helpers
    bf16 = panel.dtype
    depth = rows // (SIDE_CHIPS * CORES)

    def at(z, y, core, x):
        return ((z * SIDE_CHIPS + y) * CORES + core) * helpers + x

    def shape(*dims):
        return jax.ShapeDtypeStruct(dims, bf16)

    def gathered(shard):
        others = [
            lax.ppermute(shard, "help", [(i, i ^ d) for i in range(helpers)]) for d in distances(helpers)[1:]
        ]
        return [shard] + others

    def exchanged(to_pair, to_cross):
        cross_pairs = [(s, (s + 1) % rows if s % 2 else (s - 1) % rows) for s in range(rows)]
        cross = lax.ppermute(to_cross, "rows", cross_pairs)
        pair = lax.ppermute(to_pair, "rows", [(s, s ^ 1) for s in range(rows)])
        return pair, cross

    params = pltpu.CompilerParams(vmem_limit_bytes=24 * 1024 * 1024)

    ints = jnp.concatenate(
        [
            jnp.pad(tile_cols, ((0, 0), (0, LANES - slots))),
            jnp.pad(tile_count[None], ((0, 0), (0, LANES - row_tiles))),
            jnp.pad(row_assign[None], ((0, 0), (0, LANES - slab_size))),
            jnp.pad(send_lists[0], ((0, 0), (0, LANES - ghosts))),
        ],
        axis=0,
    )
    coefs = jnp.broadcast_to(jnp.concatenate([centers, half_widths])[:, None], (2 * volumes, LANES))
    own_panel = pl.pallas_call(
        own_blocks,
        out_shape=shape(row_tiles, vectors, side),
        in_specs=[VMEM] * 2,
        out_specs=VMEM,
        compiler_params=params,
        name="own_blocks",
    )(panel, tiles)
    base, to_pair, to_cross = pl.pallas_call(
        functools.partial(spread_panel, helpers),
        out_shape=[shape(slab_size, vectors, side)] + [shape(ghosts, vectors, side)] * 2,
        in_specs=[VMEM] * (1 + helpers),
        out_specs=[VMEM] * 3,
        compiler_params=params,
        name="spread_panel",
    )(ints, own_panel, *gathered(panel)[1:])
    pair, cross = exchanged(to_pair, to_cross)
    part_shape = jax.ShapeDtypeStruct((volumes, row_tiles, vectors, side), jnp.float32)
    product_cost = pl.CostEstimate(
        flops=4 * volumes * row_tiles * slots * side * side * vectors,
        bytes_accessed=2 * tiles.size,
        transcendentals=0,
    )
    table_shape = (5, LANES)
    part, stored, table = pl.pallas_call(
        near_first,
        out_shape=[
            part_shape,
            shape(row_tiles, vectors, side),
            jax.ShapeDtypeStruct(table_shape, jnp.int32),
        ],
        in_specs=[VMEM] * 4,
        out_specs=[VMEM] * 3,
        scratch_shapes=[
            pltpu.VMEM((slab_size + 2 * ghosts, vectors, side), bf16),
            pltpu.SMEM(table_shape, jnp.int32),
            pltpu.SemaphoreType.DMA,
        ],
        compiler_params=params,
        cost_estimate=product_cost,
        name="near_first",
    )(ints, base, pair, tiles)
    first, gram_one = pl.pallas_call(
        apply_first,
        out_shape=[
            shape(volumes, row_tiles, vectors, side),
            jax.ShapeDtypeStruct((volumes, vectors, vectors), jnp.float32),
        ],
        in_specs=[VMEM] * 6,
        out_specs=[VMEM] * 2,
        scratch_shapes=[pltpu.VMEM(part_shape.shape, jnp.float32)],
        compiler_params=params,
        name="apply_first",
    )(coefs, table, stored, cross, tiles, part)
    slab, to_pair, to_cross = pl.pallas_call(
        functools.partial(spread_field, helpers),
        out_shape=[shape(volumes, slab_size, vectors, side)] + [shape(volumes, ghosts, vectors, side)] * 2,
        in_specs=[VMEM] * (1 + helpers),
        out_specs=[VMEM] * 3,
        compiler_params=params,
        name="spread_field",
    )(table, *gathered(first))
    pair, cross = exchanged(to_pair, to_cross)
    part = pl.pallas_call(
        near_second,
        out_shape=part_shape,
        in_specs=[VMEM] * 4,
        out_specs=VMEM,
        scratch_shapes=[pltpu.VMEM((volumes, slab_size + 2 * ghosts, vectors, side), bf16)],
        compiler_params=params,
        cost_estimate=product_cost,
        name="near_second",
    )(ints, slab, pair, tiles)
    second, gram = pl.pallas_call(
        apply_second,
        out_shape=[
            shape(volumes, row_tiles, vectors, side),
            jax.ShapeDtypeStruct((vectors, 2 * volumes * vectors), jnp.float32),
        ],
        in_specs=[VMEM] * 8,
        out_specs=[VMEM] * 2,
        scratch_shapes=[pltpu.VMEM(part_shape.shape, jnp.float32)],
        compiler_params=params,
        name="apply_second",
    )(coefs, table, stored, cross, tiles, part, first, gram_one)

    near = [
        [at(z, y, c, x) for y in range(SIDE_CHIPS) for x in range(helpers)]
        for z in range(depth)
        for c in range(CORES)
    ]
    far = [
        [at(z, y, c, x) for z in range(depth) for c in range(CORES)]
        for y in range(SIDE_CHIPS)
        for x in range(helpers)
    ]
    gram = jnp.sum(summed_parts(gram, near).astype(jnp.float32), axis=0)
    gram, late = lax.optimization_barrier((gram, second))
    shards = gathered(late)
    parts = summed_parts(gram, far)
    filtered, gram = pl.pallas_call(
        functools.partial(finish, helpers, 1.0 / (row_tiles * side * helpers * rows)),
        out_shape=[
            shape(volumes, vectors, row_tiles * side),
            jax.ShapeDtypeStruct((volumes, 2, vectors, vectors), jnp.float32),
        ],
        in_specs=[VMEM] * (2 + helpers),
        out_specs=[VMEM] * 2,
        compiler_params=params,
        name="finish",
    )(table, parts, *shards)
    return filtered, gram


def solution(mesh):
    placed = (
        P(None, ("rows", "help")),
        P(None, ("rows", "help"), None, None, None),
        P(("rows", "help"), None),
        P(("rows", "help")),
        P("rows"),
        P("rows", None, None),
        P(),
        P(),
    )
    return jax.shard_map(
        per_device,
        mesh=mesh,
        in_specs=placed,
        out_specs=(P(None, None, ("rows", "help")), P()),
        check_vma=False,
    )
```
